128 devices in a mesh: segment: 4 (over x), seq: 32 (over z, y, core).
Axes of the slice: x: 4, y: 4, z: 4, core: 2. Of those that a mesh axis runs over, the one named last changes fastest.
Arguments:
- token_ids: int32 [256], P('seq'), may hold values from 0 to 511
- cached_len: int32 [2], replicated, may hold values from 128 to 786432
- embed: bfloat16 [512, 8192], P(None, 'seq'), may hold values from -6 to 6
- gain: float32 [4, 8192], P('segment'), may hold values from 0.1 to 1.9
- w_in: bfloat16 [4, 8192, 3, 8192], P('segment', None, None, 'seq'), may hold values from -0.0625 to 0.0625
- short_filter: float32 [4, 7, 3, 8192], P('segment', None, None, 'seq'), may hold values from -2.5 to 2.5
- long_filter: float32 [4, 128, 512], P('segment', None, 'seq'), may hold values from -0.5 to 0.5
- w_out: bfloat16 [4, 8192, 8192], P('segment', None, 'seq'), may hold values from -0.0625 to 0.0625
- short_cycle: bfloat16 [4, 2, 128, 3, 8192], P('segment', None, None, None, 'seq'), may hold values from -6 to 6
- long_cycle: bfloat16 [4, 2, 128, 8192], P('segment', None, None, 'seq'), may hold values from -6 to 6
Outputs:
- section_out: bfloat16 [4, 256, 8192], P('segment', None, 'seq')
- new_short_cycle: bfloat16 [4, 2, 128, 3, 8192], P('segment', None, None, None, 'seq')
- new_long_cycle: bfloat16 [4, 2, 128, 8192], P('segment', None, None, 'seq')
The draws below stay inside these ranges and needn't reach their ends.
All inputs are finite; a program needn't handle non-finite values.
Results may differ from the reference program's by a relative error of at most 0.023.
Values may be sent and summed in bfloat16 or wider, within the bound.
A program may use at most 128 MiB of HBM per device.

```python
import math
import jax
import jax.numpy as jnp
import numpy as np
from jax import lax

D = 8192
G = 512
VOCAB = 512
SHORT = 7
LONG = 128
CONTEXT = 786432
REQUESTS = 2
TOKENS = 256
NEW = 128
LAYERS = 4


def plant(result, stream_key, low, largest):
    index_at = [jax.random.randint(jax.random.fold_in(stream_key, axis), (), 0, length) for axis, length in enumerate(result.shape)]
    main_axis = result.shape.index(max(result.shape))
    next_to = index_at[:main_axis] + [(index_at[main_axis] + 1) % result.shape[main_axis]] + index_at[main_axis + 1:]
    return result.at[tuple(index_at)].set(low).at[tuple(next_to)].set(largest)


def level_of(stream_key, shape, split, smallest, top_value):
    factor_of, own = 1.0, jax.random.fold_in(stream_key, 6)
    for axis_at, shards_of in split:
        heights = jnp.exp(jax.random.uniform(jax.random.fold_in(own, axis_at), (shards_of,), jnp.float32, smallest / len(split), top_value / len(split)))
        factor_of = factor_of * jnp.repeat(heights, shape[axis_at] // shards_of).reshape([-1 if axis == axis_at else 1 for axis in range(len(shape))])
    return factor_of


def cumulative_ranks(number_of, slope):
    weights = [(1 << 20) // math.isqrt(standing ** slope) + 1 for standing in range(1, number_of + 1)]
    width = 1 + sum(weights) // (1 << 30)
    return np.cumsum(np.array([max(1, weight // width) for weight in weights]))


def skewed_ids(own_key, extent, amount, skew):
    listing = cumulative_ranks(amount, skew)
    ticket = jax.random.randint(jax.random.fold_in(own_key, 1), extent, 0, int(listing[amount - 1]))
    grade = jnp.searchsorted(jnp.asarray(listing, jnp.int32), ticket, side="right")
    return jax.random.permutation(jax.random.fold_in(own_key, 2), amount)[grade].astype(jnp.int32)


def noise(stream_key, shape, spread, most, split=(), dtype=jnp.bfloat16):
    level = level_of(stream_key, shape, split, -0.22, 0.18) if split else 1.0
    array = jax.random.normal(stream_key, shape, jnp.float32) * spread * level
    return jnp.minimum(jnp.maximum(array, -most), most).astype(dtype)


def setup_inputs(seed: int = 0) -> dict:
    arg_keys = jax.random.split(jax.random.key(seed), 11)
    token_ids = plant(skewed_ids(arg_keys[0], (TOKENS,), VOCAB, 2), jax.random.fold_in(arg_keys[0], 3), 0, VOCAB - 1).astype(jnp.int32)
    cached_len = jax.random.randint(arg_keys[1], (REQUESTS,), LONG, CONTEXT + 1).astype(jnp.int32)
    embed = noise(arg_keys[2], (VOCAB, D), 1.0, 6.0, ((1, 32),))
    gain = jnp.clip(1.0 + 0.18 * jax.random.normal(arg_keys[3], (LAYERS, D), jnp.float32), 0.1, 1.9)
    w_in = noise(arg_keys[4], (LAYERS, D, 3, D), D ** -0.5, 0.0625, ((0, 4), (3, 32)))
    short_filter = noise(arg_keys[5], (LAYERS, SHORT, 3, D), 0.4, 2.5, ((0, 4), (3, 32)), jnp.float32)
    long_filter = noise(arg_keys[6], (LAYERS, LONG, G), 0.09, 0.5, ((0, 4), (2, 32)), jnp.float32)
    w_out = noise(arg_keys[7], (LAYERS, D, D), D ** -0.5, 0.0625, ((0, 4), (2, 32)))
    short_cycle = noise(arg_keys[8], (LAYERS, REQUESTS, LONG, 3, D), 1.0, 6.0, ((0, 4), (4, 32)))
    long_cycle = noise(arg_keys[9], (LAYERS, REQUESTS, LONG, D), 1.0, 6.0, ((0, 4), (3, 32)))
    return dict(token_ids=token_ids, cached_len=cached_len, embed=embed, gain=gain, w_in=w_in, short_filter=short_filter, long_filter=long_filter, w_out=w_out, short_cycle=short_cycle, long_cycle=long_cycle)


def cycle_rows(cycle, offset):
    doubled = jnp.concatenate([cycle, cycle], axis=0)
    return lax.dynamic_slice_in_dim(doubled, offset.astype(jnp.int32), cycle.shape[0], 0)

def reference(token_ids, cached_len, embed, gain, w_in, short_filter, long_filter, w_out, short_cycle, long_cycle):
    hidden = embed[token_ids]
    section_list = []
    short_list = []
    long_list = []
    for layer in range(LAYERS):
        widened = hidden.astype(jnp.float32)
        scaling = lax.rsqrt(lax.optimization_barrier(jnp.mean(widened * widened, axis=1, keepdims=True)) + 1e-06)
        normed = (widened * scaling * gain[layer][None, :]).astype(jnp.bfloat16)
        projected = jnp.dot(normed, w_in[layer].reshape(D, 3 * D), preferred_element_type=jnp.float32)
        projected = projected.astype(jnp.bfloat16).reshape(TOKENS, 3, D)
        channel_taps = jnp.repeat(long_filter[layer], D // G, axis=1)
        mixed_parts = []
        short_cycles = []
        long_cycles = []
        for request in range(REQUESTS):
            prefix = cached_len[request]
            appended = projected[request * NEW:(request + 1) * NEW]
            extended = jnp.concatenate([cycle_rows(short_cycle[layer, request], prefix % LONG), appended], axis=0)
            wide_ext = extended.astype(jnp.float32)
            filtered = jnp.zeros((NEW, 3, D), jnp.float32)
            for tap_index in range(SHORT):
                filtered = filtered + short_filter[layer, tap_index][None] * wide_ext[LONG - tap_index:LONG - tap_index + NEW]
            product = (filtered[:, 1] * filtered[:, 2]).astype(jnp.bfloat16)
            carried = jnp.concatenate([cycle_rows(long_cycle[layer, request], prefix % LONG), product], axis=0)
            wide_carried = carried.astype(jnp.float32)
            convolved = jnp.zeros((NEW, D), jnp.float32)
            for tap_index in range(LONG):
                convolved = convolved + channel_taps[tap_index][None] * wide_carried[LONG - tap_index:LONG - tap_index + NEW]
            mixed_parts.append((filtered[:, 0] * convolved).astype(jnp.bfloat16))
            backward = (LONG - (prefix + NEW) % LONG) % LONG
            short_cycles.append(cycle_rows(extended[NEW:], backward))
            long_cycles.append(cycle_rows(carried[NEW:], backward))
        mixed = jnp.concatenate(mixed_parts, axis=0)
        added = jnp.dot(mixed, w_out[layer], preferred_element_type=jnp.float32)
        hidden = (hidden.astype(jnp.float32) + added).astype(jnp.bfloat16)
        section_list.append(hidden)
        short_list.append(jnp.stack(short_cycles))
        long_list.append(jnp.stack(long_cycles))
    return (jnp.stack(section_list), jnp.stack(short_list), jnp.stack(long_list))
```

```python
import jax
import jax.numpy as jnp
from jax import lax
from jax.experimental import pallas as pl
from jax.experimental.pallas import tpu as pltpu
from jax.sharding import PartitionSpec as P

D = 8192
SHORT = 7
LONG = 128
REQUESTS = 2
SIDE = 4
CHIPS = SIDE * SIDE
ROWS = 64
CHUNKS = 4
BLOCK = 256
WIDE = 2 * BLOCK
GROUP = 16
GROUPS = BLOCK // GROUP
TAIL = REQUESTS * LONG
TAPS = TAIL + REQUESTS * 3 * 8
PACK = TAPS + 3 * 8
LEAD = 2
MESH = pl.DeviceIdType.MESH
F32 = jnp.float32
BF16 = jnp.bfloat16


def dot(a, b):
    return jnp.dot(a, b, preferred_element_type=F32)


def folded(i):
    return i + (i // 2) * (5 - 2 * i)


def kernel(
    ids_ref,
    len_ref,
    embed_ref,
    gain_ref,
    w_in_ref,
    short_ref,
    long_ref,
    w_out_ref,
    short_cycle_ref,
    long_cycle_ref,
    section_ref,
    new_short_ref,
    new_long_ref,
    w_in,
    w_out,
    gathered,
    section_in,
    outgoing,
    acc,
    squares,
    extended,
    masked,
    toeplitz,
    toeplitz_old,
    pack,
    reversed_taps,
    keep,
    stage,
    ids_all,
    ids_own,
    embed_other,
    section_half,
    gather_send,
    gather_recv,
    hop_send,
    hop_recv,
    w_in_send,
    w_in_recv,
    w_out_send,
    w_out_recv,
    prep_send,
    prep_recv,
    keep_send,
    keep_recv,
    half_send,
    half_recv,
    ids_send,
    ids_recv,
):
    segment = lax.axis_index("segment")
    seq = lax.axis_index("seq")
    core = lax.rem(seq, 2)
    chip = seq // 2
    row_z, row_y = chip // SIDE, lax.rem(chip, SIDE)
    sibling = (segment, chip * 2 + 1 - core)

    def chip_at(k, sign):
        dz, dy = folded(k // SIDE), folded(lax.rem(k, SIDE))
        z = lax.rem(row_z + sign * dz + SIDE, SIDE)
        y = lax.rem(row_y + sign * dy + SIDE, SIDE)
        return z * SIDE + y

    def remote(src, dst, send, recv, where):
        return pltpu.make_async_remote_copy(
            src_ref=src, dst_ref=dst, send_sem=send, recv_sem=recv, device_id=where, device_id_type=MESH
        )

    def rows_of(j):
        return pl.ds(pl.multiple_of(j * WIDE, WIDE), WIDE)

    barrier = pltpu.get_barrier_semaphore()

    def greet(k, carry):
        pl.semaphore_signal(
            barrier, inc=1, device_id=(segment, k * 2 + 1 - core), device_id_type=MESH
        )
        return carry

    lax.fori_loop(0, CHIPS, greet, 0)

    @pl.when(core == 1)
    def _():
        for step in (1, 3):
            pl.semaphore_signal(
                barrier, inc=1, device_id=(lax.rem(segment + step, 4), seq), device_id_type=MESH
            )

    def w_in_local(k):
        rows = rows_of(chip_at(k, 1))
        return pltpu.make_async_copy(
            w_in_ref.at[:, rows, :], w_in.at[0, :, rows, :], w_in_recv.at[0, k]
        )

    def w_in_remote(k):
        rows = rows_of(chip_at(k, 1))
        return remote(
            w_in_ref.at[:, rows, :], w_in.at[1, :, rows, :], w_in_send.at[k], w_in_recv.at[1, k], sibling
        )

    w_out_local = pltpu.make_async_copy(w_out_ref, w_out.at[1], w_out_recv.at[1])
    w_out_remote = remote(w_out_ref, w_out.at[0], w_out_send, w_out_recv.at[0], sibling)

    def order(i):
        return lax.rem(i + 1, CHIPS)

    @pl.when(core == 0)
    def _():
        def begin(i, carry):
            w_in_local(order(i)).start()
            return carry

        lax.fori_loop(0, CHIPS, begin, 0)

    @pl.when(core == 1)
    def _():
        w_out_local.start()

    sub = lax.broadcasted_iota(jnp.int32, (8, 128), 0)
    mine = jnp.zeros((8, 128), jnp.int32)
    for i in range(8):
        mine = jnp.where(sub == i, ids_ref[i], mine)

    @pl.when(core == 0)
    def _():
        ids_own[0:8, :] = mine

    @pl.when(core == 1)
    def _():
        ids_own[8:16, :] = mine

    @pl.when(core == 0)
    def _():
        pl.semaphore_wait(barrier, CHIPS)

    @pl.when(core == 1)
    def _():
        pl.semaphore_wait(barrier, CHIPS + 2)

    ids_pair = remote(
        ids_own.at[pl.ds(8, 8)], ids_own.at[pl.ds(8, 8)], ids_send.at[CHIPS], ids_recv.at[CHIPS], sibling
    )
    embed_half = remote(embed_ref, embed_other, prep_send.at[2], prep_recv.at[2], sibling)

    def ids_to(k):
        return remote(
            ids_own, ids_all.at[chip], ids_send.at[k], ids_recv.at[chip], (segment, k * 2 + 1)
        )

    def ids_from(k):
        return remote(ids_own, ids_all.at[k], ids_send.at[k], ids_recv.at[k], sibling)

    @pl.when((segment == 0) & (core == 1))
    def _():
        ids_pair.start()

    @pl.when((segment == 0) & (core == 0))
    def _():
        ids_pair.wait_recv()

        def give(k, carry):
            ids_to(k).start()
            return carry

        lax.fori_loop(0, CHIPS, give, 0)
        embed_half.start()

    @pl.when(core == 1)
    def _():
        def begin(i, carry):
            w_in_remote(order(i)).start()
            return carry

        lax.fori_loop(0, CHIPS, begin, 0)

    @pl.when(core == 0)
    def _():
        w_out_remote.start()

    flip_from = lax.broadcasted_iota(jnp.int32, (LONG, 2 * LONG), 0)
    flip_to = lax.broadcasted_iota(jnp.int32, (LONG, 2 * LONG), 1)
    flip = (flip_from + flip_to == LONG).astype(F32).astype(BF16)
    reversed_taps[...] = dot(long_ref[...].astype(BF16), flip)
    lane_group = lax.broadcasted_iota(jnp.int32, (1, BLOCK), 1) // GROUP

    def group_columns(g):
        return pl.ds(pl.multiple_of(g * LONG, LONG), LONG)

    def expand(g, carry):
        line = jnp.broadcast_to(reversed_taps[pl.ds(g, 1), :], (LONG, 2 * LONG))
        turned = pltpu.roll(line, 0, 1, stride=1, stride_axis=0)
        toeplitz_old[:, group_columns(g)] = turned[:, :LONG].astype(BF16)
        toeplitz[core, :, group_columns(g)] = turned[:, LONG:].astype(BF16)
        return carry

    lax.fori_loop(0, GROUPS, expand, 0)

    at_row = lax.broadcasted_iota(jnp.int32, (LONG, LONG), 0)
    at_col = lax.broadcasted_iota(jnp.int32, (LONG, LONG), 1)
    last_row = lax.broadcasted_iota(jnp.int32, (8, LONG), 0)
    last_col = lax.broadcasted_iota(jnp.int32, (8, LONG), 1)
    for r in range(REQUESTS):
        prefix = len_ref[r]
        slot = ((at_row + prefix) & (LONG - 1)) == at_col
        old = dot(slot.astype(F32).astype(BF16), long_cycle_ref[r])

        def spread(g, carry):
            masked[0, group_columns(g), :] = jnp.where(lane_group == g, old, 0.0).astype(BF16)
            return carry

        lax.fori_loop(0, GROUPS, spread, 0)
        pack[core, r * LONG : (r + 1) * LONG, :] = dot(toeplitz_old[...], masked[0])
        slot = ((last_row + (prefix - 8)) & (LONG - 1)) == last_col
        pick = slot.astype(F32).astype(BF16)
        for b in range(3):
            at = TAIL + (r * 3 + b) * 8
            pack[core, at : at + 8, :] = dot(pick, short_cycle_ref[r, b])
    for b in range(3):
        for j in range(SHORT):
            at = TAPS + b * 8 + j
            pack[core, at : at + 1, :] = short_ref[j * 3 + b]
        pack[core, TAPS + b * 8 + 7 : TAPS + b * 8 + 8, :] = jnp.zeros((1, BLOCK), F32)

    pack_copy = remote(pack.at[1], pack.at[1], prep_send.at[0], prep_recv.at[0], sibling)
    toeplitz_copy = remote(toeplitz.at[1], toeplitz.at[1], prep_send.at[1], prep_recv.at[1], sibling)

    @pl.when(core == 1)
    def _():
        pack_copy.start()
        toeplitz_copy.start()

    def spread_out(src, m):
        def begin(i, carry):
            k = order(i)
            target = (segment, chip_at(k, -1) * 2 + 1 - core)
            remote(
                src, gathered.at[m, chip], gather_send.at[m, k], gather_recv.at[m, k], target
            ).start()
            return carry

        lax.fori_loop(0, CHIPS, begin, 0)

    def arrived(m, k):
        j = chip_at(k, 1)
        remote(
            section_in.at[0], gathered.at[m, j], gather_send.at[m, k], gather_recv.at[m, k], sibling
        ).wait_recv()
        return j

    def keep_copy(m):
        return remote(stage.at[m], keep.at[m], keep_send.at[m], keep_recv.at[m], sibling)

    def half_copy(m):
        return remote(
            outgoing.at[m, :, pl.ds(0, BLOCK)], section_half.at[m], half_send.at[m], half_recv.at[m], sibling
        )

    def hop_copy(m):
        return remote(
            outgoing.at[m],
            section_in.at[m],
            hop_send.at[m],
            hop_recv.at[m],
            (lax.rem(segment + 1, 4), seq),
        )

    def write_cycles():
        for r in range(REQUESTS):
            prefix = len_ref[r]
            turn = (((at_row - prefix) & (LONG - 1)) == at_col).astype(F32).astype(BF16)
            for b in range(4):
                rows = jnp.concatenate([keep[2 * r, b], keep[2 * r + 1, b]], axis=0)
                rolled = dot(turn, rows).astype(BF16)
                if b < 3:
                    new_short_ref[r, b] = rolled
                else:
                    new_long_ref[r] = rolled

    def project(m, carry):
        acc[...] = jnp.zeros_like(acc)
        squares[...] = jnp.zeros_like(squares)

        def pair(i, inner):
            for p in range(2):
                k = order(2 * i + p)
                j = arrived(m, k)

                @pl.when(m == 0)
                def _():
                    w_in_local(k).wait()
                    w_in_remote(k).wait_recv()

                wide = gathered[m, j].astype(F32)
                power = wide * wide
                squares[...] += (
                    power[:, 0:128] + power[:, 128:256] + power[:, 256:384] + power[:, 384:512]
                )
                scaled = (wide * gain_ref[:, rows_of(j)]).astype(BF16)
                for c in range(2):
                    for b in range(3):
                        acc[c * 3 + b] += dot(scaled, w_in[c, b, rows_of(j), :])
            return inner

        lax.fori_loop(0, CHIPS // 2, pair, 0)
        scale = lax.rsqrt(jnp.sum(squares[...], axis=1, keepdims=True) * (1.0 / D) + 1e-6)
        half = lax.rem(m, 2)
        request = m // 2

        @pl.when(m == 0)
        def _():
            pack_copy.wait_recv()
            toeplitz_copy.wait_recv()

        for c in range(2):
            filtered = []
            for b in range(3):
                e = c * 3 + b
                own = (acc[e] * scale).astype(BF16)
                if c == 0:
                    keep[m, b] = own
                else:
                    stage[m, b] = own

                @pl.when(half == 0)
                def _():
                    at = pl.multiple_of(TAIL + (request * 3 + b) * 8, 8)
                    extended[e, 0:8, :] = pack[c, pl.ds(at, 8), :]

                @pl.when(half == 1)
                def _():
                    extended[e, 0:8, :] = extended[e, ROWS : ROWS + 8, :]

                extended[e, 8 : 8 + ROWS, :] = own.astype(F32)
                total = jnp.zeros((ROWS, BLOCK), F32)
                for j in range(SHORT):
                    at = TAPS + b * 8 + j
                    total = total + pack[c, at : at + 1, :] * extended[e, 8 - j : 8 - j + ROWS, :]
                filtered.append(total)
            product = (filtered[1] * filtered[2]).astype(BF16)
            if c == 0:
                keep[m, 3] = product
            else:
                stage[m, 3] = product
            wide = product.astype(F32)

            def spread(g, inner):
                base = g * LONG
                here = pl.multiple_of(base + half * ROWS, ROWS)
                masked[c, pl.ds(here, ROWS), :] = jnp.where(lane_group == g, wide, 0.0).astype(BF16)

                @pl.when(half == 0)
                def _():
                    later = pl.multiple_of(base + ROWS, ROWS)
                    masked[c, pl.ds(later, ROWS), :] = jnp.zeros((ROWS, BLOCK), BF16)

                return inner

            lax.fori_loop(0, GROUPS, spread, 0)
            mine = pl.ds(pl.multiple_of(half * ROWS, ROWS), ROWS)
            past = pl.ds(pl.multiple_of(m * ROWS, ROWS), ROWS)
            convolved = pack[c, past, :] + dot(toeplitz[c, mine, :], masked[c])
            outgoing[m, :, c * BLOCK : (c + 1) * BLOCK] = (filtered[0] * convolved).astype(BF16)
        spread_out(outgoing.at[m], m)
        keep_copy(m).start()
        return carry

    lanes = lax.broadcasted_iota(jnp.int32, (ROWS, 128), 1)

    def pass_on(m):
        @pl.when(segment == 0)
        def _():
            @pl.when(m == 0)
            def _():
                def take(k, carry):
                    ids_from(k).wait_recv()
                    return carry

                lax.fori_loop(0, CHIPS, take, 0)
                embed_half.wait_recv()

            ids = ids_all[pl.ds(m * (ROWS // 16), ROWS // 16)].reshape(ROWS, 128)
            left = jnp.zeros((ROWS, BLOCK), F32)
            right = jnp.zeros((ROWS, BLOCK), F32)
            for v in range(4):
                hot = (ids == lanes + 128 * v).astype(F32).astype(BF16)
                left = left + dot(hot, embed_other[v * 128 : (v + 1) * 128, :])
                right = right + dot(hot, embed_ref[v * 128 : (v + 1) * 128, :])
            section_in[m, :, 0:BLOCK] = left.astype(BF16)
            section_in[m, :, BLOCK:WIDE] = right.astype(BF16)

        @pl.when(segment > 0)
        def _():
            hop_copy(m).wait_recv()

        spread_out(section_in.at[m], m)

    def put_out(m):
        @pl.when(m == 0)
        def _():
            w_out_local.wait()
            w_out_remote.wait_recv()

        acc[0:2] = jnp.zeros((2, ROWS, BLOCK), F32)

        def pair(i, inner):
            for p in range(2):
                j = arrived(m, order(2 * i + p))
                block = gathered[m, j]
                for c in range(2):
                    acc[c] += dot(block, w_out[c, rows_of(j), :])
            return inner

        lax.fori_loop(0, CHIPS // 2, pair, 0)
        for c in range(2):
            cols = slice(c * BLOCK, (c + 1) * BLOCK)
            outgoing[m, :, cols] = (section_in[m, :, cols].astype(F32) + acc[c]).astype(BF16)

        @pl.when(segment < 3)
        def _():
            hop_copy(m).start()

        half_copy(m).start()
        at = pl.ds(pl.multiple_of(m * ROWS, ROWS), ROWS)
        section_ref[at, :] = outgoing[m, :, BLOCK:WIDE]

    @pl.when(core == 0)
    def _():
        lax.fori_loop(0, CHUNKS, project, 0)
        write_cycles()
        for m in range(CHUNKS):
            half_copy(m).wait_recv()
            section_ref[m * ROWS : (m + 1) * ROWS, :] = section_half[m]
            keep_copy(m).wait_send()
        w_out_remote.wait_send()

    @pl.when(core == 1)
    def _():
        lead = jnp.where(segment == 0, 1, LEAD)

        def turn(i, carry):
            @pl.when(i < CHUNKS)
            def _():
                pass_on(i)

            m = i - lead

            @pl.when(m == CHUNKS - 1)
            def _():
                for n in range(CHUNKS):
                    keep_copy(n).wait_recv()
                write_cycles()

            @pl.when((m >= 0) & (m < CHUNKS))
            def _():
                put_out(m)

            return carry

        lax.fori_loop(0, CHUNKS + LEAD, turn, 0)
        for m in range(CHUNKS):
            half_copy(m).wait_send()

            @pl.when(segment < 3)
            def _():
                hop_copy(m).wait_send()

        def sent(k, carry):
            w_in_remote(k).wait_send()
            return carry

        lax.fori_loop(0, CHIPS, sent, 0)
        pack_copy.wait_send()
        toeplitz_copy.wait_send()

    def sent_chunk(i, carry):
        m, k = i // CHIPS, lax.rem(i, CHIPS)
        remote(
            section_in.at[0], gathered.at[m, chip], gather_send.at[m, k], gather_recv.at[m, k], sibling
        ).wait_send()
        return carry

    lax.fori_loop(0, CHUNKS * CHIPS, sent_chunk, 0)

    @pl.when((segment == 0) & (core == 1))
    def _():
        ids_pair.wait_send()

    @pl.when((segment == 0) & (core == 0))
    def _():
        def sent(k, carry):
            ids_to(k).wait_send()
            return carry

        lax.fori_loop(0, CHIPS, sent, 0)
        embed_half.wait_send()


def local(
    token_ids,
    cached_len,
    embed,
    gain,
    w_in,
    short_filter,
    long_filter,
    w_out,
    short_cycle,
    long_cycle,
):
    vmem = pl.BlockSpec(memory_space=pltpu.VMEM)
    smem = pl.BlockSpec(memory_space=pltpu.SMEM)
    anywhere = pl.BlockSpec(memory_space=pl.ANY)
    dma = pltpu.SemaphoreType.DMA
    section, new_short, new_long = pl.pallas_call(
        kernel,
        out_shape=(
            jax.ShapeDtypeStruct((CHUNKS * ROWS, BLOCK), BF16),
            jax.ShapeDtypeStruct((REQUESTS, 3, LONG, BLOCK), BF16),
            jax.ShapeDtypeStruct((REQUESTS, LONG, BLOCK), BF16),
        ),
        in_specs=[smem, smem, vmem, vmem, anywhere, vmem, vmem, anywhere, vmem, vmem],
        out_specs=(vmem, vmem, vmem),
        scratch_shapes=[
            pltpu.VMEM((2, 3, D, BLOCK), BF16),
            pltpu.VMEM((2, D, BLOCK), BF16),
            pltpu.VMEM((CHUNKS, CHIPS, ROWS, WIDE), BF16),
            pltpu.VMEM((CHUNKS, ROWS, WIDE), BF16),
            pltpu.VMEM((CHUNKS, ROWS, WIDE), BF16),
            pltpu.VMEM((6, ROWS, BLOCK), F32),
            pltpu.VMEM((ROWS, 128), F32),
            pltpu.VMEM((6, ROWS + 8, BLOCK), F32),
            pltpu.VMEM((2, GROUPS * LONG, BLOCK), BF16),
            pltpu.VMEM((2, LONG, GROUPS * LONG), BF16),
            pltpu.VMEM((LONG, GROUPS * LONG), BF16),
            pltpu.VMEM((2, PACK, BLOCK), F32),
            pltpu.VMEM((GROUPS, 2 * LONG), F32),
            pltpu.VMEM((CHUNKS, 4, ROWS, BLOCK), BF16),
            pltpu.VMEM((CHUNKS, 4, ROWS, BLOCK), BF16),
            pltpu.VMEM((CHIPS, 16, 128), jnp.int32),
            pltpu.VMEM((16, 128), jnp.int32),
            pltpu.VMEM((512, BLOCK), BF16),
            pltpu.VMEM((CHUNKS, ROWS, BLOCK), BF16),
            dma((CHUNKS, CHIPS)),
            dma((CHUNKS, CHIPS)),
            dma((CHUNKS,)),
            dma((CHUNKS,)),
            dma((CHIPS,)),
            dma((2, CHIPS)),
            dma,
            dma((2,)),
            dma((3,)),
            dma((3,)),
            dma((CHUNKS,)),
            dma((CHUNKS,)),
            dma((CHUNKS,)),
            dma((CHUNKS,)),
            dma((CHIPS + 1,)),
            dma((CHIPS + 1,)),
        ],
        compiler_params=pltpu.CompilerParams(
            collective_id=0, has_side_effects=True, vmem_limit_bytes=56 * 2**20
        ),
        name="layers",
    )(
        token_ids,
        cached_len,
        embed,
        gain,
        w_in[0].transpose(1, 0, 2),
        short_filter.reshape(SHORT * 3, 1, BLOCK),
        long_filter[0].T,
        w_out[0],
        short_cycle[0].transpose(0, 2, 1, 3),
        long_cycle[0],
    )
    return section[None], new_short.transpose(0, 2, 1, 3)[None], new_long[None]


def solution(mesh):
    in_specs = (
        P("seq"),
        P(),
        P(None, "seq"),
        P("segment", None),
        P("segment", None, None, "seq"),
        P("segment", None, None, "seq"),
        P("segment", None, "seq"),
        P("segment", None, "seq"),
        P("segment", None, None, None, "seq"),
        P("segment", None, None, "seq"),
    )
    out_specs = (
        P("segment", None, "seq"),
        P("segment", None, None, None, "seq"),
        P("segment", None, None, "seq"),
    )
    return jax.shard_map(local, mesh=mesh, in_specs=in_specs, out_specs=out_specs, check_vma=False)
```

```python
import jax
import jax.numpy as jnp
from jax import lax
from jax.experimental import pallas as pl
from jax.experimental.pallas import tpu as pltpu
from jax.sharding import PartitionSpec as P

D = 8192
SHORT = 7
LONG = 128
REQUESTS = 2
SIDE = 4
CHIPS = SIDE * SIDE
ROWS = 64
CHUNKS = 4
BLOCK = 256
GROUP = 16
GROUPS = BLOCK // GROUP
TAIL = REQUESTS * LONG
TAPS = TAIL + REQUESTS * 3 * 8
PACK = TAPS + 3 * 8
LEAD = 3
MESH = pl.DeviceIdType.MESH
F32 = jnp.float32
BF16 = jnp.bfloat16


def dot(a, b):
    return jnp.dot(a, b, preferred_element_type=F32)


def kernel(
    ids_ref,
    len_ref,
    embed_ref,
    gain_ref,
    w_in_ref,
    short_ref,
    long_ref,
    w_out_ref,
    short_cycle_ref,
    long_cycle_ref,
    section_ref,
    new_short_ref,
    new_long_ref,
    w_in,
    w_out,
    gathered,
    section_in,
    outgoing,
    acc,
    squares,
    extended,
    masked,
    toeplitz,
    toeplitz_old,
    pack,
    reversed_taps,
    keep,
    stage,
    ids_all,
    ids_own,
    embed_other,
    section_half,
    near_send,
    next_send,
    near_recv,
    far_send,
    far_recv,
    hop_send,
    hop_recv,
    w_in_send,
    w_in_recv,
    w_out_send,
    w_out_recv,
    prep_send,
    prep_recv,
    keep_send,
    keep_recv,
    half_send,
    half_recv,
    ids_send,
    ids_recv,
):
    segment = lax.axis_index("segment")
    seq = lax.axis_index("seq")
    core = lax.rem(seq, 2)
    chip = seq // 2
    row_z, row_y = chip // SIDE, lax.rem(chip, SIDE)
    sibling = (segment, chip * 2 + 1 - core)

    def along(c, step):
        if c == 0:
            return row_z * SIDE + lax.rem(row_y + step, SIDE)
        return lax.rem(row_z + step, SIDE) * SIDE + row_y

    places = (row_z, row_y)

    def remote(src, dst, send, recv, where):
        return pltpu.make_async_remote_copy(
            src_ref=src, dst_ref=dst, send_sem=send, recv_sem=recv, device_id=where, device_id_type=MESH
        )

    barrier = pltpu.get_barrier_semaphore()

    before = lax.rem(segment + 3, 4)
    after = lax.rem(segment + 1, 4)

    def greet(where, at, core_of):
        pl.semaphore_signal(
            barrier, inc=1, device_id=(where, at * 2 + core_of), device_id_type=MESH
        )

    near = [along(c, step) for c in range(2) for step in range(1, SIDE)]
    for at in near:
        greet(segment, at, core)

    @pl.when(core == 0)
    def _():
        for at in near + [chip]:
            greet(segment, at, 1)
            greet(before, at, 1)

    @pl.when(core == 1)
    def _():
        def greet_one(k, carry):
            greet(segment, k, 0)
            return carry

        lax.fori_loop(0, CHIPS, greet_one, 0)
        greet(before, chip, 1)

    def group(c, step):
        return lax.rem(places[c] + step, SIDE)

    def w_in_part(c, step):
        i = group(c, step)
        return w_in_ref.at[:, i, :, 0] if c == 0 else w_in_ref.at[:, :, i, 1]

    def w_in_local(c, step):
        return pltpu.make_async_copy(
            w_in_part(c, step), w_in.at[0, c, group(c, step)], w_in_recv.at[0, c, step]
        )

    def w_in_remote(c, step):
        return remote(
            w_in_part(c, step),
            w_in.at[1, c, group(c, step)],
            w_in_send.at[c, step],
            w_in_recv.at[1, c, step],
            sibling,
        )

    STEPS = [(c, step) for step in (0, 1, 3, 2) for c in range(2)]

    def w_out_part(c, i):
        return w_out_ref.at[i, :, 0] if c == 0 else w_out_ref.at[:, i, 1]

    PARTS = [(c, i) for c in range(2) for i in range(SIDE)]
    w_out_local = [
        pltpu.make_async_copy(w_out_part(c, i), w_out.at[1, c, i], w_out_recv.at[1, c, i])
        for c, i in PARTS
    ]
    w_out_remote = [
        remote(w_out_part(c, i), w_out.at[0, c, i], w_out_send.at[c, i], w_out_recv.at[0, c, i], sibling)
        for c, i in PARTS
    ]

    @pl.when(core == 0)
    def _():
        for c, step in STEPS:
            w_in_local(c, (SIDE - step) % SIDE).start()

    @pl.when(core == 1)
    def _():
        for copy in w_out_local:
            copy.start()

    sub = lax.broadcasted_iota(jnp.int32, (8, 128), 0)
    mine = jnp.zeros((8, 128), jnp.int32)
    for i in range(8):
        mine = jnp.where(sub == i, ids_ref[i], mine)

    @pl.when(core == 0)
    def _():
        ids_own[0:8, :] = mine

    @pl.when(core == 1)
    def _():
        ids_own[8:16, :] = mine

    @pl.when(core == 0)
    def _():
        pl.semaphore_wait(barrier, len(near) + CHIPS)

    @pl.when(core == 1)
    def _():
        pl.semaphore_wait(barrier, 3 * len(near) + 3)

    ids_pair = remote(
        ids_own.at[pl.ds(8, 8)], ids_own.at[pl.ds(8, 8)], ids_send.at[CHIPS], ids_recv.at[CHIPS], sibling
    )
    embed_half = remote(embed_ref, embed_other, prep_send.at[2], prep_recv.at[2], sibling)

    def ids_to(k):
        return remote(
            ids_own, ids_all.at[chip], ids_send.at[k], ids_recv.at[chip], (segment, k * 2 + 1)
        )

    def ids_from(k):
        return remote(ids_own, ids_all.at[k], ids_send.at[k], ids_recv.at[k], sibling)

    @pl.when((segment == 0) & (core == 1))
    def _():
        ids_pair.start()

    @pl.when((segment == 0) & (core == 0))
    def _():
        ids_pair.wait_recv()

        def give(k, carry):
            ids_to(k).start()
            return carry

        lax.fori_loop(0, CHIPS, give, 0)
        embed_half.start()

    @pl.when(core == 1)
    def _():
        for c, step in STEPS:
            w_in_remote(c, (SIDE - step) % SIDE).start()

    @pl.when(core == 0)
    def _():
        for copy in w_out_remote:
            copy.start()

    flip_from = lax.broadcasted_iota(jnp.int32, (LONG, 2 * LONG), 0)
    flip_to = lax.broadcasted_iota(jnp.int32, (LONG, 2 * LONG), 1)
    flip = (flip_from + flip_to == LONG).astype(F32).astype(BF16)
    reversed_taps[...] = dot(long_ref[...].astype(BF16), flip)
    lane_group = lax.broadcasted_iota(jnp.int32, (1, BLOCK), 1) // GROUP

    def group_columns(g):
        return pl.ds(pl.multiple_of(g * LONG, LONG), LONG)

    def expand(g, carry):
        masked[1, group_columns(g), :] = jnp.zeros((LONG, BLOCK), BF16)
        line = jnp.broadcast_to(reversed_taps[pl.ds(g, 1), :], (LONG, 2 * LONG))
        turned = pltpu.roll(line, 0, 1, stride=1, stride_axis=0)
        toeplitz_old[:, group_columns(g)] = turned[:, :LONG].astype(BF16)
        toeplitz[core, :, group_columns(g)] = turned[:, LONG:].astype(BF16)
        return carry

    lax.fori_loop(0, GROUPS, expand, 0)

    at_row = lax.broadcasted_iota(jnp.int32, (LONG, LONG), 0)
    at_col = lax.broadcasted_iota(jnp.int32, (LONG, LONG), 1)
    last_row = lax.broadcasted_iota(jnp.int32, (8, LONG), 0)
    last_col = lax.broadcasted_iota(jnp.int32, (8, LONG), 1)
    for r in range(REQUESTS):
        prefix = len_ref[r]
        slot = ((at_row + prefix) & (LONG - 1)) == at_col
        old = dot(slot.astype(F32).astype(BF16), long_cycle_ref[r])

        def spread(g, carry):
            masked[0, group_columns(g), :] = jnp.where(lane_group == g, old, 0.0).astype(BF16)
            return carry

        lax.fori_loop(0, GROUPS, spread, 0)
        pack[core, r * LONG : (r + 1) * LONG, :] = dot(toeplitz_old[...], masked[0])
        slot = ((last_row + (prefix - 8)) & (LONG - 1)) == last_col
        pick = slot.astype(F32).astype(BF16)
        for b in range(3):
            at = TAIL + (r * 3 + b) * 8
            pack[core, at : at + 8, :] = dot(pick, short_cycle_ref[r, b])
    for b in range(3):
        for j in range(SHORT):
            at = TAPS + b * 8 + j
            pack[core, at : at + 1, :] = short_ref[j * 3 + b]
        pack[core, TAPS + b * 8 + 7 : TAPS + b * 8 + 8, :] = jnp.zeros((1, BLOCK), F32)

    pack_copy = remote(pack.at[1], pack.at[1], prep_send.at[0], prep_recv.at[0], sibling)
    toeplitz_copy = remote(toeplitz.at[1], toeplitz.at[1], prep_send.at[1], prep_recv.at[1], sibling)

    @pl.when(core == 1)
    def _():
        pack_copy.start()
        toeplitz_copy.start()

    def near_copies(src, m, where, sems):
        return [
            remote(
                src.at[m, c],
                gathered.at[m, c, places[c], places[1 - c]],
                sems.at[m, c, step],
                near_recv.at[m, c, step],
                (where, along(c, step) * 2 + 1 - core),
            )
            for step in (1, 3, 2, 0)
            for c in range(2)
        ]

    def far_copy(m, c, step):
        block = gathered.at[m, c, places[c]]
        return remote(
            block,
            block,
            far_send.at[m, c, step],
            far_recv.at[m, c, step],
            (segment, along(1 - c, step) * 2 + core),
        )

    def pass_along(m):
        for c in range(2):
            for step in range(SIDE):
                remote(
                    outgoing.at[0, 0],
                    gathered.at[m, c, places[c], lax.rem(places[1 - c] + SIDE - step, SIDE)],
                    next_send.at[m, c, step],
                    near_recv.at[m, c, step],
                    sibling,
                ).wait_recv()
            for step in (1, 3, 2):
                far_copy(m, c, step).start()

    def collect(m, use):
        for c, step in STEPS:
            i = lax.rem(places[c] + SIDE - step, SIDE)
            if step:
                block = gathered.at[m, c, i]
                remote(block, block, far_send.at[m, c, step], far_recv.at[m, c, step], sibling).wait_recv()
            use(c, i, (SIDE - step) % SIDE, jnp.concatenate([gathered[m, c, i, k] for k in range(SIDE)], axis=1))

    def keep_copy(m):
        return remote(stage.at[m], keep.at[m], keep_send.at[m], keep_recv.at[m], sibling)

    def half_copy(m):
        return remote(
            outgoing.at[m, 0], section_half.at[m], half_send.at[m], half_recv.at[m], sibling
        )

    def hop_copy(m):
        return remote(
            outgoing.at[m],
            section_in.at[m],
            hop_send.at[m],
            hop_recv.at[m],
            (after, seq),
        )

    def write_cycles():
        for r in range(REQUESTS):
            prefix = len_ref[r]
            turn = (((at_row - prefix) & (LONG - 1)) == at_col).astype(F32).astype(BF16)
            for b in range(4):
                rows = jnp.concatenate([keep[2 * r, b], keep[2 * r + 1, b]], axis=0)
                rolled = dot(turn, rows).astype(BF16)
                if b < 3:
                    new_short_ref[r, b] = rolled
                else:
                    new_long_ref[r] = rolled

    def project(m, carry):
        acc[...] = jnp.zeros_like(acc)
        squares[...] = jnp.zeros_like(squares)

        def use(c, i, step, block):
            @pl.when(m == 0)
            def _():
                w_in_local(c, step).wait()
                w_in_remote(c, step).wait_recv()

            wide = block.astype(F32)
            power = wide * wide
            total = power[:, 0:128]
            for v in range(1, SIDE * 2):
                total = total + power[:, v * 128 : (v + 1) * 128]
            squares[...] += total
            gains = jnp.concatenate([gain_ref[i, k, 0] if c == 0 else gain_ref[k, i, 1] for k in range(SIDE)], axis=1)
            scaled = (wide * gains).astype(BF16)
            for n in range(2):
                for b in range(3):
                    weights = w_in[n, c, i, b].reshape(SIDE * BLOCK, BLOCK)
                    acc[n * 3 + b] += dot(scaled, weights)

        pass_along(m)
        collect(m, use)
        scale = lax.rsqrt(jnp.sum(squares[...], axis=1, keepdims=True) * (1.0 / D) + 1e-6)
        half = lax.rem(m, 2)
        request = m // 2

        @pl.when(m == 0)
        def _():
            pack_copy.wait_recv()
            toeplitz_copy.wait_recv()

        for c in range(2):
            filtered = []
            for b in range(3):
                e = c * 3 + b
                own = (acc[e] * scale).astype(BF16)
                if c == 0:
                    keep[m, b] = own
                else:
                    stage[m, b] = own

                @pl.when(half == 0)
                def _():
                    at = pl.multiple_of(TAIL + (request * 3 + b) * 8, 8)
                    extended[e, 0:8, :] = pack[c, pl.ds(at, 8), :]

                @pl.when(half == 1)
                def _():
                    extended[e, 0:8, :] = extended[e, ROWS : ROWS + 8, :]

                extended[e, 8 : 8 + ROWS, :] = own.astype(F32)
                total = jnp.zeros((ROWS, BLOCK), F32)
                for j in range(SHORT):
                    at = TAPS + b * 8 + j
                    total = total + pack[c, at : at + 1, :] * extended[e, 8 - j : 8 - j + ROWS, :]
                filtered.append(total)
            product = (filtered[1] * filtered[2]).astype(BF16)
            if c == 0:
                keep[m, 3] = product
            else:
                stage[m, 3] = product
            wide = product.astype(F32)

            def spread(g, inner):
                base = g * LONG
                here = pl.multiple_of(base + half * ROWS, ROWS)
                masked[c, pl.ds(here, ROWS), :] = jnp.where(lane_group == g, wide, 0.0).astype(BF16)
                return inner

            lax.fori_loop(0, GROUPS, spread, 0, unroll=4)
            mine = pl.ds(pl.multiple_of(half * ROWS, ROWS), ROWS)
            past = pl.ds(pl.multiple_of(m * ROWS, ROWS), ROWS)
            convolved = pack[c, past, :] + dot(toeplitz[c, mine, :], masked[c])
            outgoing[m, c] = (filtered[0] * convolved).astype(BF16)
        for copy in near_copies(outgoing, m, segment, near_send):
            copy.start()
        keep_copy(m).start()

        return carry

    lanes = lax.broadcasted_iota(jnp.int32, (ROWS, 128), 1)

    def pass_on(m):
        @pl.when(m == 0)
        def _():
            def take(k, carry):
                ids_from(k).wait_recv()
                return carry

            lax.fori_loop(0, CHIPS, take, 0)
            embed_half.wait_recv()

        ids = ids_all[pl.ds(m * (ROWS // 16), ROWS // 16)].reshape(ROWS, 128)
        left = jnp.zeros((ROWS, BLOCK), F32)
        right = jnp.zeros((ROWS, BLOCK), F32)
        for v in range(4):
            hot = (ids == lanes + 128 * v).astype(F32).astype(BF16)
            left = left + dot(hot, embed_other[v * 128 : (v + 1) * 128, :])
            right = right + dot(hot, embed_ref[v * 128 : (v + 1) * 128, :])
        section_in[m, 0] = left.astype(BF16)
        section_in[m, 1] = right.astype(BF16)

        for copy in near_copies(section_in, m, segment, near_send):
            copy.start()

    def put_out(m):
        @pl.when(m == 0)
        def _():
            for copy in w_out_local:
                copy.wait()
            for copy in w_out_remote:
                copy.wait_recv()

        acc[0:2] = jnp.zeros((2, ROWS, BLOCK), F32)

        def use(c, i, step, block):
            for n in range(2):
                acc[n] += dot(block, w_out[n, c, i].reshape(SIDE * BLOCK, BLOCK))

        pass_along(m)
        collect(m, use)

        @pl.when(segment > 0)
        def _():
            hop_copy(m).wait_recv()

        for c in range(2):
            outgoing[m, c] = (section_in[m, c].astype(F32) + acc[c]).astype(BF16)

        @pl.when(segment < 3)
        def _():
            for copy in near_copies(outgoing, m, after, next_send):
                copy.start()
            hop_copy(m).start()

        half_copy(m).start()
        at = pl.ds(pl.multiple_of(m * ROWS, ROWS), ROWS)
        section_ref[at, :] = outgoing[m, 1]

    @pl.when(core == 0)
    def _():
        lax.fori_loop(0, CHUNKS, project, 0)
        write_cycles()
        for m in range(CHUNKS):
            half_copy(m).wait_recv()
            section_ref[m * ROWS : (m + 1) * ROWS, :] = section_half[m]
            keep_copy(m).wait_send()
        for copy in w_out_remote:
            copy.wait_send()

    @pl.when(core == 1)
    def _():
        lead = jnp.where(segment == 0, LEAD, 0)

        def turn(i, carry):
            @pl.when((segment == 0) & (i < CHUNKS))
            def _():
                pass_on(i)

            m = i - lead

            @pl.when(m == CHUNKS - 1)
            def _():
                for n in range(CHUNKS):
                    keep_copy(n).wait_recv()
                write_cycles()

            @pl.when((m >= 0) & (m < CHUNKS))
            def _():
                put_out(m)

            return carry

        lax.fori_loop(0, CHUNKS + LEAD, turn, 0)
        for m in range(CHUNKS):
            half_copy(m).wait_send()

            @pl.when(segment < 3)
            def _():
                hop_copy(m).wait_send()

        for c, step in STEPS:
            w_in_remote(c, step).wait_send()
        pack_copy.wait_send()
        toeplitz_copy.wait_send()

    def all_sent(where, sems):
        def sent(m, carry):
            for copy in near_copies(outgoing, m, where, sems):
                copy.wait_send()
            return carry

        lax.fori_loop(0, CHUNKS, sent, 0)

    @pl.when((core == 0) | (segment == 0))
    def _():
        all_sent(segment, near_send)

    @pl.when((core == 1) & (segment < 3))
    def _():
        all_sent(after, next_send)

    def far_sent(m, carry):
        for c in range(2):
            for step in (1, 3, 2):
                far_copy(m, c, step).wait_send()
        return carry

    lax.fori_loop(0, CHUNKS, far_sent, 0)

    @pl.when((segment == 0) & (core == 1))
    def _():
        ids_pair.wait_send()

    @pl.when((segment == 0) & (core == 0))
    def _():
        def sent(k, carry):
            ids_to(k).wait_send()
            return carry

        lax.fori_loop(0, CHIPS, sent, 0)
        embed_half.wait_send()


def write_out(*refs):
    for i in range(3):
        refs[3 + i][...] = refs[i][...]


def local(
    token_ids,
    cached_len,
    embed,
    gain,
    w_in,
    short_filter,
    long_filter,
    w_out,
    short_cycle,
    long_cycle,
):
    vmem = pl.BlockSpec(memory_space=pltpu.VMEM)
    smem = pl.BlockSpec(memory_space=pltpu.SMEM)
    anywhere = pl.BlockSpec(memory_space=pl.ANY)
    dma = pltpu.SemaphoreType.DMA
    section, new_short, new_long = pl.pallas_call(
        kernel,
        out_shape=(
            jax.ShapeDtypeStruct((CHUNKS * ROWS, BLOCK), BF16),
            jax.ShapeDtypeStruct((REQUESTS, 3, LONG, BLOCK), BF16),
            jax.ShapeDtypeStruct((REQUESTS, LONG, BLOCK), BF16),
        ),
        in_specs=[smem, smem, vmem, vmem, anywhere, vmem, vmem, anywhere, vmem, vmem],
        out_specs=(vmem, vmem, vmem),
        scratch_shapes=[
            pltpu.VMEM((2, 2, SIDE, 3, SIDE, BLOCK, BLOCK), BF16),
            pltpu.VMEM((2, 2, SIDE, SIDE, BLOCK, BLOCK), BF16),
            pltpu.VMEM((CHUNKS, 2, SIDE, SIDE, ROWS, BLOCK), BF16),
            pltpu.VMEM((CHUNKS, 2, ROWS, BLOCK), BF16),
            pltpu.VMEM((CHUNKS, 2, ROWS, BLOCK), BF16),
            pltpu.VMEM((6, ROWS, BLOCK), F32),
            pltpu.VMEM((ROWS, 128), F32),
            pltpu.VMEM((6, ROWS + 8, BLOCK), F32),
            pltpu.VMEM((2, GROUPS * LONG, BLOCK), BF16),
            pltpu.VMEM((2, LONG, GROUPS * LONG), BF16),
            pltpu.VMEM((LONG, GROUPS * LONG), BF16),
            pltpu.VMEM((2, PACK, BLOCK), F32),
            pltpu.VMEM((GROUPS, 2 * LONG), F32),
            pltpu.VMEM((CHUNKS, 4, ROWS, BLOCK), BF16),
            pltpu.VMEM((CHUNKS, 4, ROWS, BLOCK), BF16),
            pltpu.VMEM((CHIPS, 16, 128), jnp.int32),
            pltpu.VMEM((16, 128), jnp.int32),
            pltpu.VMEM((512, BLOCK), BF16),
            pltpu.VMEM((CHUNKS, ROWS, BLOCK), BF16),
            dma((CHUNKS, 2, SIDE)),
            dma((CHUNKS, 2, SIDE)),
            dma((CHUNKS, 2, SIDE)),
            dma((CHUNKS, 2, SIDE)),
            dma((CHUNKS, 2, SIDE)),
            dma((CHUNKS,)),
            dma((CHUNKS,)),
            dma((2, SIDE)),
            dma((2, 2, SIDE)),
            dma((2, SIDE)),
            dma((2, 2, SIDE)),
            dma((3,)),
            dma((3,)),
            dma((CHUNKS,)),
            dma((CHUNKS,)),
            dma((CHUNKS,)),
            dma((CHUNKS,)),
            dma((CHIPS + 1,)),
            dma((CHIPS + 1,)),
        ],
        compiler_params=pltpu.CompilerParams(
            collective_id=0, has_side_effects=True, vmem_limit_bytes=56 * 2**20
        ),
        name="layers",
    )(
        token_ids,
        cached_len,
        embed,
        gain.reshape(SIDE, SIDE, 2, 1, BLOCK),
        w_in[0].transpose(1, 0, 2).reshape(3, SIDE, SIDE, 2, BLOCK, BLOCK),
        short_filter.reshape(SHORT * 3, 1, BLOCK),
        long_filter[0].T,
        w_out[0].reshape(SIDE, SIDE, 2, BLOCK, BLOCK),
        short_cycle[0].transpose(0, 2, 1, 3),
        long_cycle[0],
    )
    section, new_short, new_long = pl.pallas_call(
        write_out,
        out_shape=tuple(jax.ShapeDtypeStruct(x.shape, x.dtype) for x in (section, new_short, new_long)),
        in_specs=[vmem] * 3,
        out_specs=(vmem,) * 3,
        name="write_out",
    )(section, new_short, new_long)
    return section[None], new_short.transpose(0, 2, 1, 3)[None], new_long[None]


def solution(mesh):
    in_specs = (
        P("seq"),
        P(),
        P(None, "seq"),
        P("segment", None),
        P("segment", None, None, "seq"),
        P("segment", None, None, "seq"),
        P("segment", None, "seq"),
        P("segment", None, "seq"),
        P("segment", None, None, None, "seq"),
        P("segment", None, None, "seq"),
    )
    out_specs = (
        P("segment", None, "seq"),
        P("segment", None, None, None, "seq"),
        P("segment", None, None, "seq"),
    )
    return jax.shard_map(local, mesh=mesh, in_specs=in_specs, out_specs=out_specs, check_vma=False)
```

```python
import jax
import jax.numpy as jnp
from jax import lax
from jax.experimental import pallas as pl
from jax.experimental.pallas import tpu as pltpu
from jax.sharding import PartitionSpec as P

D = 8192
SHORT = 7
LONG = 128
REQUESTS = 2
SIDE = 4
CHIPS = SIDE * SIDE
ROWS = 64
CHUNKS = 4
BLOCK = 256
GROUP = 16
GROUPS = BLOCK // GROUP
TAIL = REQUESTS * LONG
TAPS = TAIL + REQUESTS * 3 * 8
PACK = TAPS + 3 * 8
EARLY = 4
LEAD = 2
MESH = pl.DeviceIdType.MESH
F32 = jnp.float32
BF16 = jnp.bfloat16


def dot(a, b):
    return jnp.dot(a, b, preferred_element_type=F32)


def kernel(
    ids_ref,
    len_ref,
    embed_ref,
    gain_ref,
    w_in_ref,
    short_ref,
    long_ref,
    w_out_ref,
    short_cycle_ref,
    long_cycle_ref,
    section_ref,
    new_short_ref,
    new_long_ref,
    w_in,
    w_out,
    gathered,
    section_in,
    outgoing,
    acc,
    squares,
    extended,
    masked,
    group_mask,
    toeplitz,
    toeplitz_old,
    pack,
    reversed_taps,
    keep,
    stage,
    ids_all,
    ids_own,
    embed_other,
    section_half,
    near_send,
    next_send,
    near_recv,
    far_send,
    far_recv,
    hop_send,
    hop_recv,
    w_in_send,
    w_in_recv,
    w_out_send,
    w_out_recv,
    prep_send,
    prep_recv,
    keep_send,
    keep_recv,
    half_send,
    half_recv,
    ids_send,
    ids_recv,
):
    segment = lax.axis_index("segment")
    seq = lax.axis_index("seq")
    core = lax.rem(seq, 2)
    chip = seq // 2
    row_z, row_y = chip // SIDE, lax.rem(chip, SIDE)
    sibling = (segment, chip * 2 + 1 - core)

    def along(c, step):
        if c == 0:
            return row_z * SIDE + lax.rem(row_y + step, SIDE)
        return lax.rem(row_z + step, SIDE) * SIDE + row_y

    places = (row_z, row_y)

    def remote(src, dst, send, recv, where):
        return pltpu.make_async_remote_copy(
            src_ref=src, dst_ref=dst, send_sem=send, recv_sem=recv, device_id=where, device_id_type=MESH
        )

    barrier = pltpu.get_barrier_semaphore()

    before = lax.rem(segment + 3, 4)
    after = lax.rem(segment + 1, 4)

    def greet(where, at, core_of):
        pl.semaphore_signal(
            barrier, inc=1, device_id=(where, at * 2 + core_of), device_id_type=MESH
        )

    near = [along(c, step) for c in range(2) for step in range(1, SIDE)]
    for at in near:
        greet(segment, at, core)

    @pl.when(core == 0)
    def _():
        for at in near + [chip]:
            greet(segment, at, 1)
            greet(before, at, 1)

    @pl.when(core == 1)
    def _():
        def greet_one(k, carry):
            greet(segment, k, 0)
            return carry

        lax.fori_loop(0, CHIPS, greet_one, 0)
        greet(before, chip, 1)

    def group(c, step):
        return lax.rem(places[c] + step, SIDE)

    def w_in_part(c, step):
        i = group(c, step)
        return w_in_ref.at[:, i, :, 0] if c == 0 else w_in_ref.at[:, :, i, 1]

    def w_in_local(c, step):
        return pltpu.make_async_copy(
            w_in_part(c, step), w_in.at[0, c, group(c, step)], w_in_recv.at[0, c, step]
        )

    def w_in_remote(c, step):
        return remote(
            w_in_part(c, step),
            w_in.at[1, c, group(c, step)],
            w_in_send.at[c, step],
            w_in_recv.at[1, c, step],
            sibling,
        )

    STEPS = [(c, step) for step in (0, 2, 1, 3) for c in range(2)]

    def w_out_part(c, i):
        return w_out_ref.at[i, :, 0] if c == 0 else w_out_ref.at[:, i, 1]

    PARTS = [(c, i) for c in range(2) for i in range(SIDE)]
    w_out_local = [
        pltpu.make_async_copy(w_out_part(c, i), w_out.at[1, c, i], w_out_recv.at[1, c, i])
        for c, i in PARTS
    ]
    w_out_remote = [
        remote(w_out_part(c, i), w_out.at[0, c, i], w_out_send.at[c, i], w_out_recv.at[0, c, i], sibling)
        for c, i in PARTS
    ]

    @pl.when(core == 0)
    def _():
        for c, step in STEPS:
            w_in_local(c, (SIDE - step) % SIDE).start()

    @pl.when(core == 1)
    def _():
        for copy in w_out_local:
            copy.start()

    sub = lax.broadcasted_iota(jnp.int32, (8, 128), 0)
    mine = jnp.zeros((8, 128), jnp.int32)
    for i in range(8):
        mine = jnp.where(sub == i, ids_ref[i], mine)

    @pl.when(core == 0)
    def _():
        ids_own[0:8, :] = mine

    @pl.when(core == 1)
    def _():
        ids_own[8:16, :] = mine

    @pl.when(core == 0)
    def _():
        pl.semaphore_wait(barrier, len(near) + CHIPS)

    @pl.when(core == 1)
    def _():
        pl.semaphore_wait(barrier, 3 * len(near) + 3)

    ids_pair = remote(
        ids_own.at[pl.ds(8, 8)], ids_own.at[pl.ds(8, 8)], ids_send.at[CHIPS], ids_recv.at[CHIPS], sibling
    )
    embed_half = remote(embed_ref, embed_other, prep_send.at[2], prep_recv.at[2], sibling)

    def ids_to(k):
        return remote(
            ids_own, ids_all.at[chip], ids_send.at[k], ids_recv.at[chip], (segment, k * 2 + 1)
        )

    def ids_from(k):
        return remote(ids_own, ids_all.at[k], ids_send.at[k], ids_recv.at[k], sibling)

    @pl.when((segment == 0) & (core == 1))
    def _():
        ids_pair.start()

    @pl.when((segment == 0) & (core == 0))
    def _():
        ids_pair.wait_recv()

        def give(k, carry):
            ids_to(k).start()
            return carry

        lax.fori_loop(0, CHIPS, give, 0)
        embed_half.start()

    @pl.when(core == 1)
    def _():
        for c, step in STEPS[:EARLY]:
            w_in_remote(c, (SIDE - step) % SIDE).start()

    def later_weights():
        for c, step in STEPS[EARLY:]:
            w_in_remote(c, (SIDE - step) % SIDE).start()

    @pl.when((core == 1) & (segment > 0))
    def _():
        later_weights()

    @pl.when(core == 0)
    def _():
        for copy in w_out_remote:
            copy.start()

    flip_from = lax.broadcasted_iota(jnp.int32, (LONG, 2 * LONG), 0)
    flip_to = lax.broadcasted_iota(jnp.int32, (LONG, 2 * LONG), 1)
    flip = (flip_from + flip_to == LONG).astype(F32).astype(BF16)
    reversed_taps[...] = dot(long_ref[...].astype(BF16), flip)
    lane_group = lax.broadcasted_iota(jnp.int32, (1, BLOCK), 1) // GROUP

    def group_columns(g):
        return pl.ds(pl.multiple_of(g * LONG, LONG), LONG)

    def expand(g, carry):
        group_mask[g] = jnp.broadcast_to((lane_group == g).astype(F32), (ROWS, BLOCK)).astype(BF16)
        masked[1, group_columns(g), :] = jnp.zeros((LONG, BLOCK), BF16)
        line = jnp.broadcast_to(reversed_taps[pl.ds(g, 1), :], (LONG, 2 * LONG))
        turned = pltpu.roll(line, 0, 1, stride=1, stride_axis=0)
        toeplitz_old[:, group_columns(g)] = turned[:, :LONG].astype(BF16)
        toeplitz[core, :, group_columns(g)] = turned[:, LONG:].astype(BF16)
        return carry

    lax.fori_loop(0, GROUPS, expand, 0)

    at_row = lax.broadcasted_iota(jnp.int32, (LONG, LONG), 0)
    at_col = lax.broadcasted_iota(jnp.int32, (LONG, LONG), 1)
    last_row = lax.broadcasted_iota(jnp.int32, (8, LONG), 0)
    last_col = lax.broadcasted_iota(jnp.int32, (8, LONG), 1)
    for r in range(REQUESTS):
        prefix = len_ref[r]
        slot = ((at_row + prefix) & (LONG - 1)) == at_col
        old = dot(slot.astype(F32).astype(BF16), long_cycle_ref[r])

        def spread(g, carry):
            masked[0, group_columns(g), :] = jnp.where(lane_group == g, old, 0.0).astype(BF16)
            return carry

        lax.fori_loop(0, GROUPS, spread, 0)
        pack[core, r * LONG : (r + 1) * LONG, :] = dot(toeplitz_old[...], masked[0])
        slot = ((last_row + (prefix - 8)) & (LONG - 1)) == last_col
        pick = slot.astype(F32).astype(BF16)
        for b in range(3):
            at = TAIL + (r * 3 + b) * 8
            pack[core, at : at + 8, :] = dot(pick, short_cycle_ref[r, b])
    for b in range(3):
        for j in range(SHORT):
            at = TAPS + b * 8 + j
            pack[core, at : at + 1, :] = short_ref[j * 3 + b]
        pack[core, TAPS + b * 8 + 7 : TAPS + b * 8 + 8, :] = jnp.zeros((1, BLOCK), F32)

    pack_copy = remote(pack.at[1], pack.at[1], prep_send.at[0], prep_recv.at[0], sibling)
    toeplitz_copy = remote(toeplitz.at[1], toeplitz.at[1], prep_send.at[1], prep_recv.at[1], sibling)

    @pl.when(core == 1)
    def _():
        pack_copy.start()
        toeplitz_copy.start()

    def near_copies(src, m, where, sems, halves=(0, 1)):
        return [
            remote(
                src.at[m, c],
                gathered.at[m, c, places[c], places[1 - c]],
                sems.at[m, c, step],
                near_recv.at[m, c, step],
                (where, along(c, step) * 2 + 1 - core),
            )
            for step in (2, 1, 3, 0)
            for c in halves
        ]

    def far_copy(m, c, step):
        block = gathered.at[m, c, places[c]]
        return remote(
            block,
            block,
            far_send.at[m, c, step],
            far_recv.at[m, c, step],
            (segment, along(1 - c, step) * 2 + core),
        )

    def pass_along(m):
        for c in range(2):
            for step in range(SIDE):
                remote(
                    outgoing.at[0, 0],
                    gathered.at[m, c, places[c], lax.rem(places[1 - c] + SIDE - step, SIDE)],
                    next_send.at[m, c, step],
                    near_recv.at[m, c, step],
                    sibling,
                ).wait_recv()
            for step in (2, 1, 3):
                far_copy(m, c, step).start()

    def collect(m, use):
        for c, step in STEPS:
            i = lax.rem(places[c] + SIDE - step, SIDE)
            if step:
                block = gathered.at[m, c, i]
                remote(block, block, far_send.at[m, c, step], far_recv.at[m, c, step], sibling).wait_recv()
            use(c, i, (SIDE - step) % SIDE, jnp.concatenate([gathered[m, c, i, k] for k in range(SIDE)], axis=1))

    def keep_copy(m):
        return remote(stage.at[m], keep.at[m], keep_send.at[m], keep_recv.at[m], sibling)

    def half_copy(m):
        return remote(
            outgoing.at[m, 0], section_half.at[m], half_send.at[m], half_recv.at[m], sibling
        )

    def hop_copy(m):
        return remote(
            outgoing.at[m],
            section_in.at[m],
            hop_send.at[m],
            hop_recv.at[m],
            (after, seq),
        )

    def write_cycles():
        for r in range(REQUESTS):
            prefix = len_ref[r]
            turn = (((at_row - prefix) & (LONG - 1)) == at_col).astype(F32).astype(BF16)
            for b in range(4):
                rows = jnp.concatenate([keep[2 * r, b], keep[2 * r + 1, b]], axis=0)
                rolled = dot(turn, rows).astype(BF16)
                if b < 3:
                    new_short_ref[r, b] = rolled
                else:
                    new_long_ref[r] = rolled

    def project(m, carry):
        acc[...] = jnp.zeros_like(acc)
        squares[...] = jnp.zeros_like(squares)

        def use(c, i, step, block):
            @pl.when(m == 0)
            def _():
                w_in_local(c, step).wait()
                w_in_remote(c, step).wait_recv()

            wide = block.astype(F32)
            power = wide * wide
            total = power[:, 0:128]
            for v in range(1, SIDE * 2):
                total = total + power[:, v * 128 : (v + 1) * 128]
            squares[...] += total
            gains = jnp.concatenate([gain_ref[i, k, 0] if c == 0 else gain_ref[k, i, 1] for k in range(SIDE)], axis=1)
            scaled = (wide * gains).astype(BF16)
            for n in range(2):
                for b in range(3):
                    weights = w_in[n, c, i, b].reshape(SIDE * BLOCK, BLOCK)
                    acc[n * 3 + b] += dot(scaled, weights)

        pass_along(m)
        half = lax.rem(m, 2)
        request = m // 2

        @pl.when(m == 0)
        def _():
            pack_copy.wait_recv()
            toeplitz_copy.wait_recv()

        @pl.when(half == 0)
        def _():
            for c in range(2):
                for b in range(3):
                    at = pl.multiple_of(TAIL + (request * 3 + b) * 8, 8)
                    extended[c * 3 + b, 0:8, :] = pack[c, pl.ds(at, 8), :]

        @pl.when(half == 1)
        def _():
            for e in range(6):
                extended[e, 0:8, :] = extended[e, ROWS : ROWS + 8, :]

        collect(m, use)
        scale = lax.rsqrt(jnp.sum(squares[...], axis=1, keepdims=True) * (1.0 / D) + 1e-6)
        mine = pl.ds(pl.multiple_of(half * ROWS, ROWS), ROWS)
        past = pl.ds(pl.multiple_of(m * ROWS, ROWS), ROWS)

        def filter_branch(c, b):
            e = c * 3 + b
            own = (acc[e] * scale).astype(BF16)
            (keep if c == 0 else stage)[m, b] = own
            extended[e, 8 : 8 + ROWS, :] = own.astype(F32)
            total = None
            for j in range(SHORT):
                at = TAPS + b * 8 + j
                term = pack[c, at : at + 1, :] * extended[e, 8 - j : 8 - j + ROWS, :]
                total = term if total is None else total + term
            return total

        for c in range(2):
            product = (filter_branch(c, 1) * filter_branch(c, 2)).astype(BF16)
            (keep if c == 0 else stage)[m, 3] = product
            for g in range(GROUPS):
                here = pl.multiple_of(g * LONG + half * ROWS, ROWS)
                masked[c, pl.ds(here, ROWS), :] = product * group_mask[g]
            convolved = pack[c, past, :] + dot(toeplitz[c, mine, :], masked[c])
            outgoing[m, c] = (filter_branch(c, 0) * convolved).astype(BF16)
        for copy in near_copies(outgoing, m, segment, near_send):
            copy.start()
        keep_copy(m).start()
        return carry

    lanes = lax.broadcasted_iota(jnp.int32, (ROWS, 128), 1)

    def pass_on(m):
        @pl.when(m == 0)
        def _():
            def take(k, carry):
                ids_from(k).wait_recv()
                return carry

            lax.fori_loop(0, CHIPS, take, 0)
            embed_half.wait_recv()

        ids = ids_all[pl.ds(m * (ROWS // 16), ROWS // 16)].reshape(ROWS, 128)
        left = jnp.zeros((ROWS, BLOCK), F32)
        right = jnp.zeros((ROWS, BLOCK), F32)
        for v in range(4):
            hot = (ids == lanes + 128 * v).astype(F32).astype(BF16)
            left = left + dot(hot, embed_other[v * 128 : (v + 1) * 128, :])
            right = right + dot(hot, embed_ref[v * 128 : (v + 1) * 128, :])
        section_in[m, 0] = left.astype(BF16)
        section_in[m, 1] = right.astype(BF16)

        for copy in near_copies(section_in, m, segment, near_send):
            copy.start()

    def put_out(m):
        @pl.when(m == 0)
        def _():
            for copy in w_out_local:
                copy.wait()
            for copy in w_out_remote:
                copy.wait_recv()

        acc[0:2] = jnp.zeros((2, ROWS, BLOCK), F32)

        def use(c, i, step, block):
            for n in range(2):
                acc[n] += dot(block, w_out[n, c, i].reshape(SIDE * BLOCK, BLOCK))

        pass_along(m)

        @pl.when(m == CHUNKS - 1)
        def _():
            for n in range(CHUNKS):
                keep_copy(n).wait_recv()
            write_cycles()

        collect(m, use)

        @pl.when(segment > 0)
        def _():
            hop_copy(m).wait_recv()

        for c in range(2):
            outgoing[m, c] = (section_in[m, c].astype(F32) + acc[c]).astype(BF16)

        @pl.when(segment < 3)
        def _():
            for copy in near_copies(outgoing, m, after, next_send):
                copy.start()
            hop_copy(m).start()

        half_copy(m).start()
        at = pl.ds(pl.multiple_of(m * ROWS, ROWS), ROWS)
        section_ref[at, :] = outgoing[m, 1]

    @pl.when(core == 0)
    def _():
        lax.fori_loop(0, CHUNKS, project, 0)
        write_cycles()
        for m in range(CHUNKS):
            half_copy(m).wait_recv()
            section_ref[m * ROWS : (m + 1) * ROWS, :] = section_half[m]
            keep_copy(m).wait_send()
        for copy in w_out_remote:
            copy.wait_send()

    @pl.when(core == 1)
    def _():
        lead = jnp.where(segment == 0, LEAD, 0)

        def turn(i, carry):
            @pl.when((segment == 0) & (i < CHUNKS))
            def _():
                pass_on(i)

            @pl.when((segment == 0) & (i == 0))
            def _():
                later_weights()

            m = i - lead

            @pl.when((m >= 0) & (m < CHUNKS))
            def _():
                put_out(m)

            return carry

        lax.fori_loop(0, CHUNKS + LEAD, turn, 0)
        for m in range(CHUNKS):
            half_copy(m).wait_send()

            @pl.when(segment < 3)
            def _():
                hop_copy(m).wait_send()

        for c, step in STEPS:
            w_in_remote(c, step).wait_send()
        pack_copy.wait_send()
        toeplitz_copy.wait_send()

    def all_sent(where, sems):
        def sent(m, carry):
            for copy in near_copies(outgoing, m, where, sems):
                copy.wait_send()
            return carry

        lax.fori_loop(0, CHUNKS, sent, 0)

    @pl.when((core == 0) | (segment == 0))
    def _():
        all_sent(segment, near_send)

    @pl.when((core == 1) & (segment < 3))
    def _():
        all_sent(after, next_send)

    def far_sent(m, carry):
        for c in range(2):
            for step in (1, 3, 2):
                far_copy(m, c, step).wait_send()
        return carry

    lax.fori_loop(0, CHUNKS, far_sent, 0)

    @pl.when((segment == 0) & (core == 1))
    def _():
        ids_pair.wait_send()

    @pl.when((segment == 0) & (core == 0))
    def _():
        def sent(k, carry):
            ids_to(k).wait_send()
            return carry

        lax.fori_loop(0, CHIPS, sent, 0)
        embed_half.wait_send()


def write_out(*refs):
    for i in range(3):
        refs[3 + i][...] = refs[i][...]


def local(
    token_ids,
    cached_len,
    embed,
    gain,
    w_in,
    short_filter,
    long_filter,
    w_out,
    short_cycle,
    long_cycle,
):
    vmem = pl.BlockSpec(memory_space=pltpu.VMEM)
    smem = pl.BlockSpec(memory_space=pltpu.SMEM)
    anywhere = pl.BlockSpec(memory_space=pl.ANY)
    dma = pltpu.SemaphoreType.DMA
    section, new_short, new_long = pl.pallas_call(
        kernel,
        out_shape=(
            jax.ShapeDtypeStruct((CHUNKS * ROWS, BLOCK), BF16),
            jax.ShapeDtypeStruct((REQUESTS, 3, LONG, BLOCK), BF16),
            jax.ShapeDtypeStruct((REQUESTS, LONG, BLOCK), BF16),
        ),
        in_specs=[smem, smem, vmem, vmem, anywhere, vmem, vmem, anywhere, vmem, vmem],
        out_specs=(vmem, vmem, vmem),
        scratch_shapes=[
            pltpu.VMEM((2, 2, SIDE, 3, SIDE, BLOCK, BLOCK), BF16),
            pltpu.VMEM((2, 2, SIDE, SIDE, BLOCK, BLOCK), BF16),
            pltpu.VMEM((CHUNKS, 2, SIDE, SIDE, ROWS, BLOCK), BF16),
            pltpu.VMEM((CHUNKS, 2, ROWS, BLOCK), BF16),
            pltpu.VMEM((CHUNKS, 2, ROWS, BLOCK), BF16),
            pltpu.VMEM((6, ROWS, BLOCK), F32),
            pltpu.VMEM((ROWS, 128), F32),
            pltpu.VMEM((6, ROWS + 8, BLOCK), F32),
            pltpu.VMEM((2, GROUPS * LONG, BLOCK), BF16),
            pltpu.VMEM((GROUPS, ROWS, BLOCK), BF16),
            pltpu.VMEM((2, LONG, GROUPS * LONG), BF16),
            pltpu.VMEM((LONG, GROUPS * LONG), BF16),
            pltpu.VMEM((2, PACK, BLOCK), F32),
            pltpu.VMEM((GROUPS, 2 * LONG), F32),
            pltpu.VMEM((CHUNKS, 4, ROWS, BLOCK), BF16),
            pltpu.VMEM((CHUNKS, 4, ROWS, BLOCK), BF16),
            pltpu.VMEM((CHIPS, 16, 128), jnp.int32),
            pltpu.VMEM((16, 128), jnp.int32),
            pltpu.VMEM((512, BLOCK), BF16),
            pltpu.VMEM((CHUNKS, ROWS, BLOCK), BF16),
            dma((CHUNKS, 2, SIDE)),
            dma((CHUNKS, 2, SIDE)),
            dma((CHUNKS, 2, SIDE)),
            dma((CHUNKS, 2, SIDE)),
            dma((CHUNKS, 2, SIDE)),
            dma((CHUNKS,)),
            dma((CHUNKS,)),
            dma((2, SIDE)),
            dma((2, 2, SIDE)),
            dma((2, SIDE)),
            dma((2, 2, SIDE)),
            dma((3,)),
            dma((3,)),
            dma((CHUNKS,)),
            dma((CHUNKS,)),
            dma((CHUNKS,)),
            dma((CHUNKS,)),
            dma((CHIPS + 1,)),
            dma((CHIPS + 1,)),
        ],
        compiler_params=pltpu.CompilerParams(
            collective_id=0, has_side_effects=True, vmem_limit_bytes=56 * 2**20
        ),
        name="layers",
    )(
        token_ids,
        cached_len,
        embed,
        gain.reshape(SIDE, SIDE, 2, 1, BLOCK),
        w_in[0].transpose(1, 0, 2).reshape(3, SIDE, SIDE, 2, BLOCK, BLOCK),
        short_filter.reshape(SHORT * 3, 1, BLOCK),
        long_filter[0].T,
        w_out[0].reshape(SIDE, SIDE, 2, BLOCK, BLOCK),
        short_cycle[0].transpose(0, 2, 1, 3),
        long_cycle[0],
    )
    section, new_short, new_long = pl.pallas_call(
        write_out,
        out_shape=tuple(jax.ShapeDtypeStruct(x.shape, x.dtype) for x in (section, new_short, new_long)),
        in_specs=[vmem] * 3,
        out_specs=(vmem,) * 3,
        name="write_out",
    )(section, new_short, new_long)
    return section[None], new_short.transpose(0, 2, 1, 3)[None], new_long[None]


def solution(mesh):
    in_specs = (
        P("seq"),
        P(),
        P(None, "seq"),
        P("segment", None),
        P("segment", None, None, "seq"),
        P("segment", None, None, "seq"),
        P("segment", None, "seq"),
        P("segment", None, "seq"),
        P("segment", None, None, None, "seq"),
        P("segment", None, None, "seq"),
    )
    out_specs = (
        P("segment", None, "seq"),
        P("segment", None, None, None, "seq"),
        P("segment", None, None, "seq"),
    )
    return jax.shard_map(local, mesh=mesh, in_specs=in_specs, out_specs=out_specs, check_vma=False)
```

```python
import jax
import jax.numpy as jnp
from jax import lax
from jax.experimental import pallas as pl
from jax.experimental.pallas import tpu as pltpu
from jax.sharding import PartitionSpec as P

D = 8192
SHORT = 7
LONG = 128
REQUESTS = 2
SIDE = 4
CHIPS = SIDE * SIDE
ROWS = 64
CHUNKS = 4
BLOCK = 256
GROUP = 16
GROUPS = BLOCK // GROUP
TAIL = REQUESTS * LONG
TAPS = TAIL + REQUESTS * 3 * 8
PACK = TAPS + 3 * 8
EARLY = 4
LEAD = 2
MESH = pl.DeviceIdType.MESH
F32 = jnp.float32
BF16 = jnp.bfloat16


def dot(a, b):
    return jnp.dot(a, b, preferred_element_type=F32)


def kernel(
    ids_ref,
    len_ref,
    embed_ref,
    gain_ref,
    w_in_ref,
    short_ref,
    long_ref,
    w_out_ref,
    short_cycle_ref,
    long_cycle_ref,
    section_ref,
    new_short_ref,
    new_long_ref,
    w_in,
    w_out,
    gathered,
    section_in,
    outgoing,
    acc,
    squares,
    extended,
    masked,
    group_mask,
    toeplitz,
    toeplitz_old,
    pack,
    reversed_taps,
    keep,
    stage,
    ids_all,
    ids_own,
    embed_other,
    section_half,
    near_send,
    next_send,
    near_recv,
    far_send,
    far_recv,
    hop_send,
    hop_recv,
    w_in_send,
    w_in_recv,
    w_out_send,
    w_out_recv,
    prep_send,
    prep_recv,
    keep_send,
    keep_recv,
    half_send,
    half_recv,
    ids_send,
    ids_recv,
):
    segment = lax.axis_index("segment")
    seq = lax.axis_index("seq")
    core = lax.rem(seq, 2)
    chip = seq // 2
    row_z, row_y = chip // SIDE, lax.rem(chip, SIDE)
    sibling = (segment, chip * 2 + 1 - core)

    def along(c, step):
        if c == 0:
            return row_z * SIDE + lax.rem(row_y + step, SIDE)
        return lax.rem(row_z + step, SIDE) * SIDE + row_y

    places = (row_z, row_y)

    def remote(src, dst, send, recv, where):
        return pltpu.make_async_remote_copy(
            src_ref=src, dst_ref=dst, send_sem=send, recv_sem=recv, device_id=where, device_id_type=MESH
        )

    barrier = pltpu.get_barrier_semaphore()

    before = lax.rem(segment + 3, 4)
    after = lax.rem(segment + 1, 4)

    def greet(where, at, core_of):
        pl.semaphore_signal(
            barrier, inc=1, device_id=(where, at * 2 + core_of), device_id_type=MESH
        )

    near = [along(c, step) for c in range(2) for step in range(1, SIDE)]
    for at in near:
        greet(segment, at, core)

    @pl.when(core == 0)
    def _():
        for at in near + [chip]:
            greet(segment, at, 1)
            greet(before, at, 1)

    @pl.when(core == 1)
    def _():
        def greet_one(k, carry):
            greet(segment, k, 0)
            return carry

        lax.fori_loop(0, CHIPS, greet_one, 0)
        greet(before, chip, 1)

    def group(c, step):
        return lax.rem(places[c] + step, SIDE)

    def w_in_part(c, step):
        i = group(c, step)
        return w_in_ref.at[:, i, :, 0] if c == 0 else w_in_ref.at[:, :, i, 1]

    def w_in_local(c, step):
        return pltpu.make_async_copy(
            w_in_part(c, step), w_in.at[0, c, group(c, step)], w_in_recv.at[0, c, step]
        )

    def w_in_remote(c, step):
        return remote(
            w_in_part(c, step),
            w_in.at[1, c, group(c, step)],
            w_in_send.at[c, step],
            w_in_recv.at[1, c, step],
            sibling,
        )

    STEPS = [(c, step) for step in (0, 2, 1, 3) for c in range(2)]

    def w_out_part(c, i):
        return w_out_ref.at[i, :, 0] if c == 0 else w_out_ref.at[:, i, 1]

    PARTS = [(c, i) for c in range(2) for i in range(SIDE)]
    w_out_local = [
        pltpu.make_async_copy(w_out_part(c, i), w_out.at[1, c, i], w_out_recv.at[1, c, i])
        for c, i in PARTS
    ]
    w_out_remote = [
        remote(w_out_part(c, i), w_out.at[0, c, i], w_out_send.at[c, i], w_out_recv.at[0, c, i], sibling)
        for c, i in PARTS
    ]

    @pl.when(core == 0)
    def _():
        for c, step in STEPS:
            w_in_local(c, (SIDE - step) % SIDE).start()

    @pl.when(core == 1)
    def _():
        for copy in w_out_local:
            copy.start()

    sub = lax.broadcasted_iota(jnp.int32, (8, 128), 0)
    mine = jnp.zeros((8, 128), jnp.int32)
    for i in range(8):
        mine = jnp.where(sub == i, ids_ref[i], mine)

    @pl.when(core == 0)
    def _():
        ids_own[0:8, :] = mine

    @pl.when(core == 1)
    def _():
        ids_own[8:16, :] = mine

    @pl.when(core == 0)
    def _():
        pl.semaphore_wait(barrier, len(near) + CHIPS)

    @pl.when(core == 1)
    def _():
        pl.semaphore_wait(barrier, 3 * len(near) + 3)

    ids_pair = remote(
        ids_own.at[pl.ds(8, 8)], ids_own.at[pl.ds(8, 8)], ids_send.at[CHIPS], ids_recv.at[CHIPS], sibling
    )
    embed_half = remote(embed_ref, embed_other, prep_send.at[2], prep_recv.at[2], sibling)

    def ids_to(k):
        return remote(
            ids_own, ids_all.at[chip], ids_send.at[k], ids_recv.at[chip], (segment, k * 2 + 1)
        )

    def ids_from(k):
        return remote(ids_own, ids_all.at[k], ids_send.at[k], ids_recv.at[k], sibling)

    @pl.when((segment == 0) & (core == 1))
    def _():
        ids_pair.start()

    @pl.when((segment == 0) & (core == 0))
    def _():
        ids_pair.wait_recv()

        def give(k, carry):
            ids_to(k).start()
            return carry

        lax.fori_loop(0, CHIPS, give, 0)
        embed_half.start()

    @pl.when(core == 1)
    def _():
        for c, step in STEPS[:EARLY]:
            w_in_remote(c, (SIDE - step) % SIDE).start()

    def later_weights():
        for c, step in STEPS[EARLY:]:
            w_in_remote(c, (SIDE - step) % SIDE).start()

    @pl.when((core == 1) & (segment > 0))
    def _():
        later_weights()

    @pl.when(core == 0)
    def _():
        for copy in w_out_remote:
            copy.start()

    flip_from = lax.broadcasted_iota(jnp.int32, (LONG, 2 * LONG), 0)
    flip_to = lax.broadcasted_iota(jnp.int32, (LONG, 2 * LONG), 1)
    flip = (flip_from + flip_to == LONG).astype(F32).astype(BF16)
    reversed_taps[...] = dot(long_ref[...].astype(BF16), flip)
    lane_group = lax.broadcasted_iota(jnp.int32, (1, BLOCK), 1) // GROUP

    def group_columns(g):
        return pl.ds(pl.multiple_of(g * LONG, LONG), LONG)

    def expand(g, carry):
        group_mask[g] = jnp.broadcast_to((lane_group == g).astype(F32), (ROWS, BLOCK)).astype(BF16)
        masked[1, group_columns(g), :] = jnp.zeros((LONG, BLOCK), BF16)
        line = jnp.broadcast_to(reversed_taps[pl.ds(g, 1), :], (LONG, 2 * LONG))
        turned = pltpu.roll(line, 0, 1, stride=1, stride_axis=0)
        toeplitz_old[:, group_columns(g)] = turned[:, :LONG].astype(BF16)
        toeplitz[core, :, group_columns(g)] = turned[:, LONG:].astype(BF16)
        return carry

    lax.fori_loop(0, GROUPS, expand, 0)

    at_row = lax.broadcasted_iota(jnp.int32, (LONG, LONG), 0)
    at_col = lax.broadcasted_iota(jnp.int32, (LONG, LONG), 1)
    last_row = lax.broadcasted_iota(jnp.int32, (8, LONG), 0)
    last_col = lax.broadcasted_iota(jnp.int32, (8, LONG), 1)
    for r in range(REQUESTS):
        prefix = len_ref[r]
        slot = ((at_row + prefix) & (LONG - 1)) == at_col
        old = dot(slot.astype(F32).astype(BF16), long_cycle_ref[r])

        def spread(g, carry):
            masked[0, group_columns(g), :] = jnp.where(lane_group == g, old, 0.0).astype(BF16)
            return carry

        lax.fori_loop(0, GROUPS, spread, 0)
        pack[core, r * LONG : (r + 1) * LONG, :] = dot(toeplitz_old[...], masked[0])
        slot = ((last_row + (prefix - 8)) & (LONG - 1)) == last_col
        pick = slot.astype(F32).astype(BF16)
        for b in range(3):
            at = TAIL + (r * 3 + b) * 8
            pack[core, at : at + 8, :] = dot(pick, short_cycle_ref[r, b])
    for b in range(3):
        for j in range(SHORT):
            at = TAPS + b * 8 + j
            pack[core, at : at + 1, :] = short_ref[j * 3 + b]
        pack[core, TAPS + b * 8 + 7 : TAPS + b * 8 + 8, :] = jnp.zeros((1, BLOCK), F32)

    pack_copy = remote(pack.at[1], pack.at[1], prep_send.at[0], prep_recv.at[0], sibling)
    toeplitz_copy = remote(toeplitz.at[1], toeplitz.at[1], prep_send.at[1], prep_recv.at[1], sibling)

    @pl.when(core == 1)
    def _():
        pack_copy.start()
        toeplitz_copy.start()

    def near_copies(src, m, where, sems, halves=(0, 1)):
        return [
            remote(
                src.at[m, c],
                gathered.at[m, c, places[c], places[1 - c]],
                sems.at[m, c, step],
                near_recv.at[m, c, step],
                (where, along(c, step) * 2 + 1 - core),
            )
            for step in (2, 1, 3, 0)
            for c in halves
        ]

    def far_copy(m, c, step):
        block = gathered.at[m, c, places[c]]
        return remote(
            block,
            block,
            far_send.at[m, c, step],
            far_recv.at[m, c, step],
            (segment, along(1 - c, step) * 2 + core),
        )

    def pass_along(m):
        for c in range(2):
            for step in range(SIDE):
                remote(
                    outgoing.at[0, 0],
                    gathered.at[m, c, places[c], lax.rem(places[1 - c] + SIDE - step, SIDE)],
                    next_send.at[m, c, step],
                    near_recv.at[m, c, step],
                    sibling,
                ).wait_recv()
            for step in (2, 1, 3):
                far_copy(m, c, step).start()

    def collect(m, use):
        for c, step in STEPS:
            i = lax.rem(places[c] + SIDE - step, SIDE)
            if step:
                block = gathered.at[m, c, i]
                remote(block, block, far_send.at[m, c, step], far_recv.at[m, c, step], sibling).wait_recv()
            use(c, i, (SIDE - step) % SIDE, jnp.concatenate([gathered[m, c, i, k] for k in range(SIDE)], axis=1))

    def keep_copy(m):
        return remote(stage.at[m], keep.at[m], keep_send.at[m], keep_recv.at[m], sibling)

    def half_copy(m):
        return remote(
            outgoing.at[m, 0], section_half.at[m], half_send.at[m], half_recv.at[m], sibling
        )

    def hop_copy(m):
        return remote(
            outgoing.at[m],
            section_in.at[m],
            hop_send.at[m],
            hop_recv.at[m],
            (after, seq),
        )

    def write_cycles():
        for r in range(REQUESTS):
            prefix = len_ref[r]
            turn = (((at_row - prefix) & (LONG - 1)) == at_col).astype(F32).astype(BF16)
            for b in range(4):
                rows = jnp.concatenate([keep[2 * r, b], keep[2 * r + 1, b]], axis=0)
                rolled = dot(turn, rows).astype(BF16)
                if b < 3:
                    new_short_ref[r, b] = rolled
                else:
                    new_long_ref[r] = rolled

    def project(m, carry):
        acc[...] = jnp.zeros_like(acc)
        squares[...] = jnp.zeros_like(squares)

        def use(c, i, step, block):
            @pl.when(m == 0)
            def _():
                w_in_local(c, step).wait()
                w_in_remote(c, step).wait_recv()

            wide = block.astype(F32)
            power = wide * wide
            total = power[:, 0:128]
            for v in range(1, SIDE * 2):
                total = total + power[:, v * 128 : (v + 1) * 128]
            squares[...] += total
            gains = jnp.concatenate([gain_ref[i, k, 0] if c == 0 else gain_ref[k, i, 1] for k in range(SIDE)], axis=1)
            scaled = (wide * gains).astype(BF16)
            for n in range(2):
                for b in range(3):
                    weights = w_in[n, c, i, b].reshape(SIDE * BLOCK, BLOCK)
                    acc[n * 3 + b] += dot(scaled, weights)

        pass_along(m)
        half = lax.rem(m, 2)
        request = m // 2

        @pl.when(m == 0)
        def _():
            pack_copy.wait_recv()
            toeplitz_copy.wait_recv()

        @pl.when(half == 0)
        def _():
            for c in range(2):
                for b in range(3):
                    at = pl.multiple_of(TAIL + (request * 3 + b) * 8, 8)
                    extended[c * 3 + b, 0:8, :] = pack[c, pl.ds(at, 8), :]

        @pl.when(half == 1)
        def _():
            for e in range(6):
                extended[e, 0:8, :] = extended[e, ROWS : ROWS + 8, :]

        collect(m, use)
        scale = lax.rsqrt(jnp.sum(squares[...], axis=1, keepdims=True) * (1.0 / D) + 1e-6)
        mine = pl.ds(pl.multiple_of(half * ROWS, ROWS), ROWS)
        past = pl.ds(pl.multiple_of(m * ROWS, ROWS), ROWS)

        def filter_branch(c, b):
            e = c * 3 + b
            own = (acc[e] * scale).astype(BF16)
            (keep if c == 0 else stage)[m, b] = own
            extended[e, 8 : 8 + ROWS, :] = own.astype(F32)
            total = None
            for j in range(SHORT):
                at = TAPS + b * 8 + j
                term = pack[c, at : at + 1, :] * extended[e, 8 - j : 8 - j + ROWS, :]
                total = term if total is None else total + term
            return total

        for c in range(2):
            product = (filter_branch(c, 1) * filter_branch(c, 2)).astype(BF16)
            (keep if c == 0 else stage)[m, 3] = product
            for g in range(GROUPS):
                here = pl.multiple_of(g * LONG + half * ROWS, ROWS)
                masked[c, pl.ds(here, ROWS), :] = product * group_mask[g]
            convolved = pack[c, past, :] + dot(toeplitz[c, mine, :], masked[c])
            outgoing[m, c] = (filter_branch(c, 0) * convolved).astype(BF16)
        for copy in near_copies(outgoing, m, segment, near_send):
            copy.start()
        keep_copy(m).start()
        return carry

    lanes = lax.broadcasted_iota(jnp.int32, (ROWS, 128), 1)

    def pass_on(m):
        @pl.when(m == 0)
        def _():
            def take(k, carry):
                ids_from(k).wait_recv()
                return carry

            lax.fori_loop(0, CHIPS, take, 0)
            embed_half.wait_recv()

        ids = ids_all[pl.ds(m * (ROWS // 16), ROWS // 16)].reshape(ROWS, 128)
        left = jnp.zeros((ROWS, BLOCK), F32)
        right = jnp.zeros((ROWS, BLOCK), F32)
        for v in range(4):
            hot = (ids == lanes + 128 * v).astype(F32).astype(BF16)
            left = left + dot(hot, embed_other[v * 128 : (v + 1) * 128, :])
            right = right + dot(hot, embed_ref[v * 128 : (v + 1) * 128, :])
        section_in[m, 0] = left.astype(BF16)
        section_in[m, 1] = right.astype(BF16)

        for copy in near_copies(section_in, m, segment, near_send):
            copy.start()

    def put_out(m):
        @pl.when(m == 0)
        def _():
            for copy in w_out_local:
                copy.wait()
            for copy in w_out_remote:
                copy.wait_recv()

        acc[0:2] = jnp.zeros((2, ROWS, BLOCK), F32)

        def use(c, i, step, block):
            for n in range(2):
                acc[n] += dot(block, w_out[n, c, i].reshape(SIDE * BLOCK, BLOCK))

        pass_along(m)

        @pl.when(m == CHUNKS - 1)
        def _():
            for n in range(CHUNKS):
                keep_copy(n).wait_recv()
            write_cycles()

        collect(m, use)

        @pl.when(segment > 0)
        def _():
            hop_copy(m).wait_recv()

        for c in range(2):
            outgoing[m, c] = (section_in[m, c].astype(F32) + acc[c]).astype(BF16)

        @pl.when(segment < 3)
        def _():
            for copy in near_copies(outgoing, m, after, next_send):
                copy.start()
            hop_copy(m).start()

        half_copy(m).start()
        at = pl.ds(pl.multiple_of(m * ROWS, ROWS), ROWS)
        section_ref[at, :] = outgoing[m, 1]

    @pl.when(core == 0)
    def _():
        lax.fori_loop(0, CHUNKS, project, 0)
        write_cycles()
        for m in range(CHUNKS):
            half_copy(m).wait_recv()
            section_ref[m * ROWS : (m + 1) * ROWS, :] = section_half[m]
            keep_copy(m).wait_send()
        for copy in w_out_remote:
            copy.wait_send()

    @pl.when(core == 1)
    def _():
        lead = jnp.where(segment == 0, LEAD, 0)

        def turn(i, carry):
            @pl.when((segment == 0) & (i < CHUNKS))
            def _():
                pass_on(i)

            @pl.when((segment == 0) & (i == 0))
            def _():
                later_weights()

            m = i - lead

            @pl.when((m >= 0) & (m < CHUNKS))
            def _():
                put_out(m)

            return carry

        lax.fori_loop(0, CHUNKS + LEAD, turn, 0)
        for m in range(CHUNKS):
            half_copy(m).wait_send()

            @pl.when(segment < 3)
            def _():
                hop_copy(m).wait_send()

        for c, step in STEPS:
            w_in_remote(c, step).wait_send()
        pack_copy.wait_send()
        toeplitz_copy.wait_send()

    def all_sent(where, sems):
        def sent(m, carry):
            for copy in near_copies(outgoing, m, where, sems):
                copy.wait_send()
            return carry

        lax.fori_loop(0, CHUNKS, sent, 0)

    @pl.when((core == 0) | (segment == 0))
    def _():
        all_sent(segment, near_send)

    @pl.when((core == 1) & (segment < 3))
    def _():
        all_sent(after, next_send)

    def far_sent(m, carry):
        for c in range(2):
            for step in (1, 3, 2):
                far_copy(m, c, step).wait_send()
        return carry

    lax.fori_loop(0, CHUNKS, far_sent, 0)

    @pl.when((segment == 0) & (core == 1))
    def _():
        ids_pair.wait_send()

    @pl.when((segment == 0) & (core == 0))
    def _():
        def sent(k, carry):
            ids_to(k).wait_send()
            return carry

        lax.fori_loop(0, CHIPS, sent, 0)
        embed_half.wait_send()


def write_out(*refs):
    for i in range(3):
        refs[3 + i][...] = refs[i][...]


def local(
    token_ids,
    cached_len,
    embed,
    gain,
    w_in,
    short_filter,
    long_filter,
    w_out,
    short_cycle,
    long_cycle,
):
    vmem = pl.BlockSpec(memory_space=pltpu.VMEM)
    smem = pl.BlockSpec(memory_space=pltpu.SMEM)
    anywhere = pl.BlockSpec(memory_space=pl.ANY)
    dma = pltpu.SemaphoreType.DMA
    section, new_short, new_long = pl.pallas_call(
        kernel,
        out_shape=(
            pltpu.VMEM((CHUNKS * ROWS, BLOCK), BF16),
            pltpu.VMEM((REQUESTS, 3, LONG, BLOCK), BF16),
            pltpu.VMEM((REQUESTS, LONG, BLOCK), BF16),
        ),
        in_specs=[smem, smem, vmem, vmem, anywhere, vmem, vmem, anywhere, vmem, vmem],
        out_specs=(vmem, vmem, vmem),
        scratch_shapes=[
            pltpu.VMEM((2, 2, SIDE, 3, SIDE, BLOCK, BLOCK), BF16),
            pltpu.VMEM((2, 2, SIDE, SIDE, BLOCK, BLOCK), BF16),
            pltpu.VMEM((CHUNKS, 2, SIDE, SIDE, ROWS, BLOCK), BF16),
            pltpu.VMEM((CHUNKS, 2, ROWS, BLOCK), BF16),
            pltpu.VMEM((CHUNKS, 2, ROWS, BLOCK), BF16),
            pltpu.VMEM((6, ROWS, BLOCK), F32),
            pltpu.VMEM((ROWS, 128), F32),
            pltpu.VMEM((6, ROWS + 8, BLOCK), F32),
            pltpu.VMEM((2, GROUPS * LONG, BLOCK), BF16),
            pltpu.VMEM((GROUPS, ROWS, BLOCK), BF16),
            pltpu.VMEM((2, LONG, GROUPS * LONG), BF16),
            pltpu.VMEM((LONG, GROUPS * LONG), BF16),
            pltpu.VMEM((2, PACK, BLOCK), F32),
            pltpu.VMEM((GROUPS, 2 * LONG), F32),
            pltpu.VMEM((CHUNKS, 4, ROWS, BLOCK), BF16),
            pltpu.VMEM((CHUNKS, 4, ROWS, BLOCK), BF16),
            pltpu.VMEM((CHIPS, 16, 128), jnp.int32),
            pltpu.VMEM((16, 128), jnp.int32),
            pltpu.VMEM((512, BLOCK), BF16),
            pltpu.VMEM((CHUNKS, ROWS, BLOCK), BF16),
            dma((CHUNKS, 2, SIDE)),
            dma((CHUNKS, 2, SIDE)),
            dma((CHUNKS, 2, SIDE)),
            dma((CHUNKS, 2, SIDE)),
            dma((CHUNKS, 2, SIDE)),
            dma((CHUNKS,)),
            dma((CHUNKS,)),
            dma((2, SIDE)),
            dma((2, 2, SIDE)),
            dma((2, SIDE)),
            dma((2, 2, SIDE)),
            dma((3,)),
            dma((3,)),
            dma((CHUNKS,)),
            dma((CHUNKS,)),
            dma((CHUNKS,)),
            dma((CHUNKS,)),
            dma((CHIPS + 1,)),
            dma((CHIPS + 1,)),
        ],
        compiler_params=pltpu.CompilerParams(
            collective_id=0, has_side_effects=True, vmem_limit_bytes=56 * 2**20
        ),
        name="layers",
    )(
        token_ids,
        cached_len,
        embed,
        gain.reshape(SIDE, SIDE, 2, 1, BLOCK),
        w_in[0].transpose(1, 0, 2).reshape(3, SIDE, SIDE, 2, BLOCK, BLOCK),
        short_filter.reshape(SHORT * 3, 1, BLOCK),
        long_filter[0].T,
        w_out[0].reshape(SIDE, SIDE, 2, BLOCK, BLOCK),
        short_cycle[0].transpose(0, 2, 1, 3),
        long_cycle[0],
    )
    section, new_short, new_long = pl.pallas_call(
        write_out,
        out_shape=tuple(jax.ShapeDtypeStruct(x.shape, x.dtype) for x in (section, new_short, new_long)),
        in_specs=[vmem] * 3,
        out_specs=(vmem,) * 3,
        name="write_out",
    )(section, new_short, new_long)
    return section[None], new_short.transpose(0, 2, 1, 3)[None], new_long[None]


def solution(mesh):
    in_specs = (
        P("seq"),
        P(),
        P(None, "seq"),
        P("segment", None),
        P("segment", None, None, "seq"),
        P("segment", None, None, "seq"),
        P("segment", None, "seq"),
        P("segment", None, "seq"),
        P("segment", None, None, None, "seq"),
        P("segment", None, None, "seq"),
    )
    out_specs = (
        P("segment", None, "seq"),
        P("segment", None, None, None, "seq"),
        P("segment", None, None, "seq"),
    )
    return jax.shard_map(local, mesh=mesh, in_specs=in_specs, out_specs=out_specs, check_vma=False)
```
